512 devices in a mesh: mode: 32 (over x, y), orb: 16 (over z, core).
Axes of the slice: x: 4, y: 8, z: 8, core: 2. Of those that a mesh axis runs over, the one named last changes fastest.
Arguments:
- correlators: float32 [512, 2, 256, 256], P('mode', None, 'orb'), may hold values from -6 to 6
- density: float32 [2, 256, 256], P(None, 'orb'), may hold values from -6 to 6
- bare_hamiltonian: float32 [2, 256, 256], P(None, 'orb'), may hold values from -0.375 to 0.375
- coupling: float32 [512], P('mode'), may hold values from -0.25 to 0.25
- propagator: float32 [512, 512], P('mode'), may hold values from -0.25 to 0.25
Outputs:
- correlators_out: float32 [512, 2, 256, 256], P('mode', None, 'orb')
- density_out: float32 [2, 256, 256], P(None, 'orb')
The draws below stay inside these ranges and needn't reach their ends.
All inputs are finite; a program needn't handle non-finite values.
Results may differ from the reference program's by a relative error of at most 0.0001.
Values sent between devices are 32-bit elements; how exact they have to be, the bound alone decides.
A program may use at most 64 MiB of HBM per device.

```python
import math
import jax
import jax.numpy as jnp
from jax import lax

MODES = 512
NO = 256


def levels(stream_key, dims, shards, least, largest):
    gain = 1.0
    for dim, blocks in shards:
        draws = jax.random.uniform(jax.random.fold_in(jax.random.fold_in(stream_key, 6), dim), (blocks,), jnp.float32, least / len(shards), largest / len(shards))
        gain = gain * jnp.repeat(jnp.exp(draws), dims[dim] // blocks).reshape((-1,) + (1,) * (len(dims) - 1 - dim))
    return gain


def noise(stream_key, shape, deviation, reach, split=(), held_as=jnp.bfloat16):
    gain = levels(stream_key, shape, split, -0.22, 0.18) if split else 1.0
    values = jax.random.normal(stream_key, shape, jnp.float32) * deviation * gain
    return jnp.minimum(jnp.maximum(values, -reach), reach).astype(held_as)


def setup_inputs(seed: int = 0) -> dict:
    arg_keys = jax.random.split(jax.random.key(seed), 6)
    return {
        "correlators": noise(arg_keys[0], (MODES, 2, NO, NO), 1.0, 6.0, ((0, 32), (2, 16)), jnp.float32),
        "density": noise(arg_keys[1], (2, NO, NO), 1.0, 6.0, ((1, 16),), jnp.float32),
        "bare_hamiltonian": noise(arg_keys[2], (2, NO, NO), NO ** -0.5, 0.375, ((1, 16),), jnp.float32),
        "coupling": noise(arg_keys[3], (MODES,), MODES ** -0.5, 0.25, ((0, 32),), jnp.float32),
        "propagator": noise(arg_keys[4], (MODES, MODES), MODES ** -0.5, 0.25, ((0, 32),), jnp.float32),
    }


time_step = 0.1
field_weight = 0.0625


def contract(form, first, second):
    return jnp.einsum(form, first, second, precision=lax.Precision.HIGHEST)


def left_product(matrix, stack):
    real = contract('ij,mjk->mik', matrix[0], stack[:, 0]) - contract('ij,mjk->mik', matrix[1], stack[:, 1])
    imag = contract('ij,mjk->mik', matrix[0], stack[:, 1]) + contract('ij,mjk->mik', matrix[1], stack[:, 0])
    return jnp.stack([real, imag], axis=1)


def right_product(stack, matrix):
    real = contract('mij,jk->mik', stack[:, 0], matrix[0]) - contract('mij,jk->mik', stack[:, 1], matrix[1])
    imag = contract('mij,jk->mik', stack[:, 0], matrix[1]) + contract('mij,jk->mik', stack[:, 1], matrix[0])
    return jnp.stack([real, imag], axis=1)


def reference(correlators, density, bare_hamiltonian, coupling, propagator):
    block = math.gcd(MODES, 64)

    def substep(stacks, dens, hamil):
        shaped = stacks.reshape(MODES // block, block, 2, NO, NO)
        weights = coupling.reshape(MODES // block, block)

        def advance(pair):
            stack, weight = pair
            commut = left_product(hamil, stack) - right_product(stack, hamil)
            turned = jnp.stack([commut[:, 1], -commut[:, 0]], axis=1)
            return stack + time_step * turned + time_step * weight[:, None, None, None] * dens[None]

        updated = lax.map(advance, (shaped, weights)).reshape(MODES, 2, NO, NO)
        collision = contract('m,mcij->cij', coupling, updated)
        dens = dens + time_step * collision
        return updated, dens, bare_hamiltonian + field_weight * dens

    hamil = bare_hamiltonian + field_weight * density
    stacks, dens = correlators, density
    for turn in range(2):
        stacks, dens, hamil = substep(stacks, dens, hamil)
    stacks = contract('mn,nx->mx', propagator, stacks.reshape(MODES, -1)).reshape(MODES, 2, NO, NO)
    stacks, dens, hamil = substep(stacks, dens, hamil)
    return stacks, dens
```

```python
import functools

import jax
import jax.numpy as jnp
from jax import lax
from jax.experimental import pallas as pl
from jax.experimental.pallas import tpu as pltpu
from jax.sharding import PartitionSpec as P

MESH = pl.DeviceIdType.MESH
time_step = 0.1
field_weight = 0.0625
LANES = 128
CORES = 2
F32 = jnp.float32
BF16 = jnp.bfloat16


def split(value):
    high = value.astype(BF16)
    return high, (value - high.astype(F32)).astype(BF16)


def dot(first, second):
    return jnp.dot(first, second, preferred_element_type=F32)


def dot3(first, second):
    return dot(first[0], second[0]) + (dot(first[0], second[1]) + dot(first[1], second[0]))


def wait_for(ref, sem):
    pltpu.make_async_copy(ref, ref, sem).wait()


def kernel(
    dims,
    gin, dens, bare, coup, prop,
    out, dout,
    stage, got, abuf, ah, al, hb, zbuf, sd, mixed, back, stage2, whole, final, summed, hl, hr,
    send, recv,
):
    nx, ny, nz, rows, size = dims
    nmode, norb = nx * ny, nz * CORES
    modes = nmode * norb
    half = norb // 2
    mu, om = lax.axis_index("mode"), lax.axis_index("orb")
    px, py = mu // ny, mu % ny
    pz, core = om // CORES, om % CORES
    other = 1 - core
    pair = pz * CORES + other

    def push(src, dst, index, target):
        pltpu.make_async_remote_copy(
            src_ref=src, dst_ref=dst, send_sem=send.at[index], recv_sem=recv.at[index],
            device_id=target, device_id_type=MESH,
        ).start()

    def each(count, body):
        def step(k, carry):
            body(k)
            return carry
        lax.fori_loop(1, count, step, 0)

    barrier = pltpu.get_barrier_semaphore()

    def greet_mode(k):
        pl.semaphore_signal(barrier, inc=1, device_id=((mu + k) % nmode, om), device_id_type=MESH)

    def greet_orb(k):
        pl.semaphore_signal(barrier, inc=1, device_id=(mu, (om + k) % norb), device_id_type=MESH)

    each(nmode, greet_mode)
    each(norb, greet_orb)

    abuf[core, mu, :, :modes] = prop[pl.ds(pl.multiple_of(core * half, half), half), :]
    lines = lax.broadcasted_iota(jnp.int32, (half, LANES), 0)
    tile = jnp.zeros((half, LANES), F32)
    for j in range(half):
        tile = jnp.where(lines == j, coup[core * half + j], tile)
    abuf[core, mu, :, modes:] = tile
    for part in range(2):
        hb[part, pz, core] = bare[part] + field_weight * dens[part]
        hb[2 + part, pz, core] = dens[part]

    pl.semaphore_wait(barrier, nmode + norb - 2)

    def send_prop_y(k):
        push(abuf.at[core, mu], abuf.at[core, mu], 0, (px * ny + (py + k) % ny, om))

    each(ny, send_prop_y)

    stage[...] = jnp.swapaxes(gin[...], 0, 1)

    def send_entries(k):
        nu = (mu + k) % nmode
        push(stage.at[nu], got.at[mu], 3, (nu, om))

    each(nmode, send_entries)

    def send_fields(k):
        target = (pz + k) % nz
        push(hb.at[:, pz, core], hb.at[:, pz, core], 4, (mu, target * CORES + core))

    each(nz, send_fields)
    got[mu] = stage[mu]

    wait_for(abuf.at[0, pl.ds(0, ny - 1)], recv.at[0])
    group = pl.ds(pl.multiple_of(px * ny, ny), ny)

    def send_prop_x(k):
        push(abuf.at[core, group], abuf.at[core, group], 1, ((px + k) % nx * ny + py, om))

    each(nx, send_prop_x)
    wait_for(abuf.at[0, pl.ds(0, (nx - 1) * ny)], recv.at[1])
    push(abuf.at[core], abuf.at[core], 2, (mu, pair))
    wait_for(hb.at[:, pl.ds(0, nz - 1), 0], recv.at[4])
    push(hb.at[:, :, core], hb.at[:, :, core], 5, (mu, pair))

    def matrix(part):
        return hb[part].reshape(size, size)

    def store_h(step, real, imag):
        rh, rl = split(time_step * real)
        ih, il = split(time_step * imag)
        for level, (r, i) in enumerate(((rh, ih), (rl, il))):
            hl[step, level, :size, :size] = r
            hl[step, level, size:, size:] = r
            hl[step, level, :size, size:] = -i
            hl[step, level, size:, :size] = i
            hr[step, level, :size, :size] = r
            hr[step, level, size:, size:] = r
            hr[step, level, :size, size:] = i
            hr[step, level, size:, :size] = -i

    def turn(step, real, imag):
        rh, rl = split(real)
        ih, il = split(imag)
        left = dot3(
            (hl[step, 0], hl[step, 1]),
            (jnp.concatenate([rh, ih], 0), jnp.concatenate([rl, il], 0)),
        )
        right = dot3(
            (jnp.concatenate([rh, ih], 1), jnp.concatenate([rl, il], 1)),
            (hr[step, 0], hr[step, 1]),
        )
        return (
            real + (left[size:] - right[:, size:]),
            imag - (left[:size] - right[:, :size]),
        )

    wait_for(hb.at[:, :, 0], recv.at[5])
    store_h(0, matrix(0), matrix(1))

    wait_for(abuf.at[0], recv.at[2])

    def unpack(k, carry):
        block = jnp.concatenate([abuf[0, k, :, :modes], abuf[1, k, :, :modes]], 0)
        high, low = split(block)
        where = pl.ds(pl.multiple_of(k * norb, norb), norb)
        ah[where, :] = high
        al[where, :] = low
        return carry

    lax.fori_loop(0, nmode, unpack, 0)
    weights = jnp.concatenate(
        [abuf[0, :, :, modes:][:, None], abuf[1, :, :, modes:][:, None]], 1
    ).reshape(modes, LANES)
    own = prop[pl.ds(om, 1), :]

    wait_for(got.at[pl.ds(0, nmode - 1)], recv.at[3])
    entries = got[...].reshape(modes, size)
    wide = jnp.concatenate([weights] * (-(-size // LANES)), 1)[:, :size]
    s_row = jnp.sum(wide * entries, axis=0, keepdims=True)
    mixed[...] = dot3((ah[...], al[...]), split(entries))
    d_row = jnp.sum(wide * mixed[...], axis=0, keepdims=True)
    zbuf[pz] = jnp.concatenate([s_row, d_row, jnp.zeros((6, size), F32)], 0)

    def send_sums_z(k):
        push(zbuf.at[pz], zbuf.at[pz], 6, (mu, (pz + k) % nz * CORES + core))

    each(nz, send_sums_z)

    def send_mixed(k):
        nu = (mu + k) % nmode
        push(mixed.at[pl.ds(pl.multiple_of(nu * norb, norb), norb)], back.at[mu], 10, (nu, om))

    each(nmode, send_mixed)
    back[mu] = mixed[pl.ds(pl.multiple_of(mu * norb, norb), norb), :]

    wait_for(zbuf.at[pl.ds(0, nz - 1)], recv.at[6])
    lines = zbuf[...]
    sd[core, mu, 0] = lines[:, 0, :]
    sd[core, mu, 1] = lines[:, 1, :]

    def send_sums_y(k):
        push(sd.at[core, mu], sd.at[core, mu], 7, (px * ny + (py + k) % ny, om))

    each(ny, send_sums_y)

    column = jnp.sum(weights[:, :1] * (ah[...].astype(F32) + al[...].astype(F32)), axis=0, keepdims=True)
    both = jnp.concatenate([own, column, jnp.zeros((6, modes), F32)], 0)
    products = jnp.dot(both, weights, precision=lax.Precision.HIGHEST, preferred_element_type=F32)
    e_own = products[0:1, 0:1]
    f_all = products[1:2, 0:1]
    c_all = jnp.sum(weights * weights, axis=0, keepdims=True)[:, :1]
    c_own = coup[om]

    wait_for(sd.at[0, pl.ds(0, ny - 1)], recv.at[7])

    def send_sums_x(k):
        push(sd.at[core, group], sd.at[core, group], 8, ((px + k) % nx * ny + py, om))

    each(nx, send_sums_x)

    wait_for(back.at[pl.ds(0, nmode - 1)], recv.at[10])
    stage2[...] = jnp.swapaxes(back[...], 0, 1).reshape(norb, 2, rows, size)

    def send_matrix(k):
        target = (om + k) % norb
        push(stage2.at[target], whole.at[:, om], 11, (mu, target))

    each(norb, send_matrix)
    whole[:, om] = stage2[om]

    wait_for(sd.at[0, pl.ds(0, (nx - 1) * ny)], recv.at[8])
    push(sd.at[core], sd.at[core], 9, (mu, pair))
    wait_for(sd.at[0], recv.at[9])
    for side in range(2):
        for part in range(2):
            block = sd[side, part * rows : (part + 1) * rows].reshape(rows, 2 * nz, size)
            block = jnp.swapaxes(block, 0, 1).reshape(2, nz, rows, size)
            summed[0, part, :, side] = block[0]
            summed[1, part, :, side] = block[1]

    def total(which, part):
        return summed[which, part].reshape(size, size)

    dens0 = (matrix(2), matrix(3))
    source = tuple(total(0, part) for part in range(2))
    fields = tuple(matrix(part) for part in range(2))
    densities = [dens0]
    for step in range(2):
        source = turn(step, *source)
        source = tuple(source[p] + (c_all * time_step) * densities[step][p] for p in range(2))
        densities.append(tuple(densities[step][p] + time_step * source[p] for p in range(2)))
        fields = tuple(fields[p] + (field_weight * time_step) * source[p] for p in range(2))
        store_h(step + 1, *fields)

    wait_for(whole.at[:, pl.ds(0, norb - 1)], recv.at[11])
    state = (whole[0].reshape(size, size), whole[1].reshape(size, size))
    for step in range(3):
        weight = e_own if step < 2 else c_own
        state = turn(step, *state)
        state = tuple(state[p] + (weight * time_step) * densities[step][p] for p in range(2))
    for part in range(2):
        final[part] = state[part].reshape(norb, rows, size)

    def send_result(k):
        target = (om + k) % norb
        push(final.at[:, target], out.at[om], 12, (mu, target))

    each(norb, send_result)
    out[om] = final[:, om]

    chain = tuple(total(1, part) for part in range(2))
    for step in range(3):
        weight = f_all if step < 2 else c_all
        chain = turn(step, *chain)
        chain = tuple(chain[p] + (weight * time_step) * densities[step][p] for p in range(2))
    for part in range(2):
        summed[0, part] = (densities[2][part] + time_step * chain[part]).reshape(nz, CORES, rows, size)
    for part in range(2):
        dout[part] = summed[0, part, pz, core]

    wait_for(out.at[pl.ds(0, norb - 1)], recv.at[12])
    wait_for(abuf.at[0, pl.ds(0, ny - 1)], send.at[0])
    wait_for(abuf.at[0, pl.ds(0, (nx - 1) * ny)], send.at[1])
    wait_for(abuf.at[0], send.at[2])
    wait_for(got.at[pl.ds(0, nmode - 1)], send.at[3])
    wait_for(hb.at[:, pl.ds(0, nz - 1), 0], send.at[4])
    wait_for(hb.at[:, :, 0], send.at[5])
    wait_for(zbuf.at[pl.ds(0, nz - 1)], send.at[6])
    wait_for(sd.at[0, pl.ds(0, ny - 1)], send.at[7])
    wait_for(sd.at[0, pl.ds(0, (nx - 1) * ny)], send.at[8])
    wait_for(sd.at[0], send.at[9])
    wait_for(back.at[pl.ds(0, nmode - 1)], send.at[10])
    wait_for(whole.at[:, pl.ds(0, norb - 1)], send.at[11])
    wait_for(out.at[pl.ds(0, norb - 1)], send.at[12])


def build(mesh, nx, ny):
    def on_device(correlators, density, bare_hamiltonian, coupling, propagator):
        local, _, rows, size = correlators.shape
        nmode, norb = mesh.shape["mode"], mesh.shape["orb"]
        nz = norb // CORES
        modes = nmode * norb
        vmem = pl.BlockSpec(memory_space=pltpu.VMEM)
        return pl.pallas_call(
            functools.partial(kernel, (nx, ny, nz, rows, size)),
            out_shape=(
                jax.ShapeDtypeStruct(correlators.shape, F32),
                jax.ShapeDtypeStruct(density.shape, F32),
            ),
            in_specs=[vmem, vmem, vmem, pl.BlockSpec(memory_space=pltpu.SMEM), vmem],
            out_specs=(vmem, vmem),
            scratch_shapes=[
                pltpu.VMEM((nmode, norb, size), F32),
                pltpu.VMEM((nmode, norb, size), F32),
                pltpu.VMEM((2, nmode, norb // 2, modes + LANES), F32),
                pltpu.VMEM((modes, modes), BF16),
                pltpu.VMEM((modes, modes), BF16),
                pltpu.VMEM((4, nz, CORES, rows, size), F32),
                pltpu.VMEM((nz, 8, size), F32),
                pltpu.VMEM((2, nmode, 2, nz, size), F32),
                pltpu.VMEM((modes, size), F32),
                pltpu.VMEM((nmode, norb, size), F32),
                pltpu.VMEM((norb, 2, rows, size), F32),
                pltpu.VMEM((2, norb, rows, size), F32),
                pltpu.VMEM((2, norb, rows, size), F32),
                pltpu.VMEM((2, 2, nz, CORES, rows, size), F32),
                pltpu.VMEM((3, 2, 2 * size, 2 * size), BF16),
                pltpu.VMEM((3, 2, 2 * size, 2 * size), BF16),
                pltpu.SemaphoreType.DMA((13,)),
                pltpu.SemaphoreType.DMA((13,)),
            ],
            compiler_params=pltpu.CompilerParams(
                collective_id=0, has_side_effects=True, vmem_limit_bytes=50 * 1024 * 1024
            ),
        )(
            correlators.reshape(local, 2 * rows, size),
            density, bare_hamiltonian, coupling, propagator,
        )

    in_specs = (
        P("mode", None, "orb", None),
        P(None, "orb", None),
        P(None, "orb", None),
        P("mode"),
        P("mode", None),
    )
    out_specs = (P("mode", None, "orb", None), P(None, "orb", None))
    return jax.shard_map(
        on_device, mesh=mesh, in_specs=in_specs, out_specs=out_specs, check_vma=False
    )


def solution(mesh):
    return build(mesh, 4, mesh.shape["mode"] // 4)
```

```python
import functools

import jax
import jax.numpy as jnp
from jax import lax
from jax.experimental import pallas as pl
from jax.experimental.pallas import tpu as pltpu
from jax.sharding import PartitionSpec as P

MESH = pl.DeviceIdType.MESH
time_step = 0.1
field_weight = 0.0625
LANES = 128
CORES = 2
F32 = jnp.float32
BF16 = jnp.bfloat16


def split(value):
    high = value.astype(BF16)
    return high, (value - high.astype(F32)).astype(BF16)


def dot(first, second):
    return jnp.dot(first, second, preferred_element_type=F32)


def dot3(first, second):
    return dot(first[0], second[0]) + (dot(first[0], second[1]) + dot(first[1], second[0]))


def wait_for(ref, sem):
    pltpu.make_async_copy(ref, ref, sem).wait()


def kernel(
    dims,
    gin_hbm, dens_hbm, bare_hbm, coup, prop_hbm,
    out, dout,
    gin, dens, bare, prop, stage, got, abuf, ah, al, hb, zbuf, shares, shared, sd, mixed, back, stage2, whole, final, summed, hl, hr,
    send, recv, load,
):
    nx, ny, nz, rows, size = dims
    nmode, norb = nx * ny, nz * CORES
    modes = nmode * norb
    half = norb // 2
    cols = size // 2
    PROP_Y, PROP_X, PROP_C = 0, 0, nx
    base = 2 * nx
    ENTRY, MIXED, WHOLE = base, base + 2, base + 4
    FIELD_Z, FIELD_C, RESULT, FIRST = base + 6, base + 7, base + 8, base + 9
    SUM_Z, SUM_Y, SUM_X, SUM_C = base + 10, base + 12, base + 14, base + 16
    mu, om = lax.axis_index("mode"), lax.axis_index("orb")
    px, py = mu // ny, mu % ny
    pz, core = om // CORES, om % CORES
    other = 1 - core
    pair = pz * CORES + other

    def push(src, dst, index, target):
        pltpu.make_async_remote_copy(
            src_ref=src, dst_ref=dst, send_sem=send.at[index], recv_sem=recv.at[index],
            device_id=target, device_id_type=MESH,
        ).start()

    pending = []

    def arrive(ref, index):
        wait_for(ref, recv.at[index])

    def each(count, body):
        def step(k, carry):
            body(k)
            return carry
        lax.fori_loop(1, count, step, 0)

    loads = [
        pltpu.make_async_copy(src, dst, load.at[i])
        for i, (src, dst) in enumerate(
            ((prop_hbm, prop), (gin_hbm, gin), (bare_hbm, bare), (dens_hbm, dens))
        )
    ]
    for copy in loads:
        copy.start()

    barrier = pltpu.get_barrier_semaphore()

    def greet_mode(k):
        pl.semaphore_signal(barrier, inc=1, device_id=((mu + k) % nmode, om), device_id_type=MESH)

    def greet_orb(k):
        pl.semaphore_signal(barrier, inc=1, device_id=(mu, (om + k) % norb), device_id_type=MESH)

    each(nmode, greet_mode)
    each(norb, greet_orb)

    loads[0].wait()
    abuf[core, mu, :, :modes] = prop[pl.ds(pl.multiple_of(core * half, half), half), :]
    lines = lax.broadcasted_iota(jnp.int32, (half, LANES), 0)
    tile = jnp.zeros((half, LANES), F32)
    for j in range(half):
        tile = jnp.where(lines == j, coup[core * half + j], tile)
    abuf[core, mu, :, modes:] = tile
    loads[2].wait()
    loads[3].wait()
    for part in range(2):
        hb[part, pz, core] = bare[part] + field_weight * dens[part]
        hb[2 + part, pz, core] = dens[part]
    loads[1].wait()
    for h in range(2):
        stage[h] = jnp.swapaxes(gin[:, :, h * cols : (h + 1) * cols], 0, 1)

    share = coup[0] * gin[0]
    for i in range(1, norb):
        share = share + coup[i] * gin[i]
    shares[...] = share[:, None, :]

    pl.semaphore_wait(barrier, nmode + norb - 2)

    def send_prop_y(k):
        push(abuf.at[core, mu], abuf.at[core, mu], PROP_Y, (px * ny + (py + k) % ny, om))

    each(ny, send_prop_y)
    pending.append((abuf.at[0, pl.ds(0, ny - 1)], PROP_Y))

    def send_entries(h, k):
        nu = (mu + k) % nmode
        push(stage.at[h, nu], got.at[h, mu], ENTRY + h, (nu, om))

    def send_fields(k):
        target = (pz + k) % nz
        push(hb.at[:, pz, core], hb.at[:, pz, core], FIELD_Z, (mu, target * CORES + core))

    each(nmode, functools.partial(send_entries, 0))
    pending.append((got.at[0, pl.ds(0, nmode - 1)], ENTRY))

    def span_of(d):
        return pl.ds(pl.multiple_of((px - d + nx) % nx * ny, ny), ny)

    order = [0, 1] + list(range(nx - 1, 1, -1))
    group = span_of(0)

    def cross(d):
        push(abuf.at[core, span_of(d)], abuf.at[core, span_of(d)], PROP_C + d, (mu, pair))
        pending.append((abuf.at[0, pl.ds(0, ny)], PROP_C + d))

    arrive(abuf.at[0, pl.ds(0, ny - 1)], PROP_Y)
    for d in order[1:]:
        push(abuf.at[core, group], abuf.at[core, group], PROP_X + d, ((px + d) % nx * ny + py, om))
        pending.append((abuf.at[0, pl.ds(0, ny)], PROP_X + d))
    cross(0)
    each(nmode, functools.partial(send_entries, 1))
    pending.append((got.at[1, pl.ds(0, nmode - 1)], ENTRY + 1))

    def send_share(k):
        nu = (mu + k) % nmode
        push(shares.at[nu], shared.at[mu], FIRST, (nu, om))

    each(nmode, send_share)
    pending.append((shared.at[pl.ds(0, nmode - 1)], FIRST))
    each(nz, send_fields)
    pending.append((hb.at[:, pl.ds(0, nz - 1), 0], FIELD_Z))
    shared[mu] = shares[mu]
    for h in range(2):
        got[h, mu] = stage[h, mu]
    for d in order[1:]:
        arrive(abuf.at[0, pl.ds(0, ny)], PROP_X + d)
        cross(d)

    def matrix(part):
        return hb[part].reshape(size, size)

    def store_h(step, real, imag):
        rh, rl = split(time_step * real)
        ih, il = split(time_step * imag)
        for level, (r, i) in enumerate(((rh, ih), (rl, il))):
            hl[step, level, :size, :size] = r
            hl[step, level, size:, size:] = r
            hl[step, level, :size, size:] = -i
            hl[step, level, size:, :size] = i
            hr[step, level, :size, :size] = r
            hr[step, level, size:, size:] = r
            hr[step, level, :size, size:] = i
            hr[step, level, size:, :size] = -i

    def turn(step, real, imag):
        rh, rl = split(real)
        ih, il = split(imag)
        left = dot3(
            (hl[step, 0], hl[step, 1]),
            (jnp.concatenate([rh, ih], 0), jnp.concatenate([rl, il], 0)),
        )
        right = dot3(
            (jnp.concatenate([rh, ih], 1), jnp.concatenate([rl, il], 1)),
            (hr[step, 0], hr[step, 1]),
        )
        return (
            real + (left[size:] - right[:, size:]),
            imag - (left[:size] - right[:, :size]),
        )

    def unpack(d):
        arrive(abuf.at[0, pl.ds(0, ny)], PROP_C + d)

        def step(j, carry):
            k = (px - d + nx) % nx * ny + j
            block = jnp.concatenate([abuf[0, k, :, :modes], abuf[1, k, :, :modes]], 0)
            high, low = split(block)
            where = pl.ds(pl.multiple_of(k * norb, norb), norb)
            ah[where, :] = high
            al[where, :] = low
            return carry

        lax.fori_loop(0, ny, step, 0)

    def mix(h):
        high, low = split(got[h].reshape(modes, cols))
        span = ny * norb
        for d in order:
            if h == 0:
                unpack(d)
            first = (px - d + nx) % nx
            where = pl.ds(pl.multiple_of(first * span, span), span)
            mixed[h, where, :] = dot3((ah[where, :], al[where, :]), (high, low))

            def send_mixed(k, first=first):
                nu = first * ny + (py + k) % ny
                rows_of = pl.ds(pl.multiple_of(nu * norb, norb), norb)
                push(mixed.at[h, rows_of], back.at[h, mu], MIXED + h, (nu, om))

            if d:
                send_mixed(0)
            each(ny, send_mixed)
        back[h, mu] = mixed[h, pl.ds(pl.multiple_of(mu * norb, norb), norb), :]
        pending.append((back.at[h, pl.ds(0, nmode - 1)], MIXED + h))

    def sums_z(which, row):
        zbuf[which, pz] = row

        def send_sums(k):
            target = (mu, (pz + k) % nz * CORES + core)
            push(zbuf.at[which, pz], zbuf.at[which, pz], SUM_Z + which, target)

        each(nz, send_sums)
        pending.append((zbuf.at[which, pl.ds(0, nz - 1)], SUM_Z + which))

    def sums_y(which):
        arrive(zbuf.at[which, pl.ds(0, nz - 1)], SUM_Z + which)
        sd[which, core, mu] = zbuf[which][:, 0, :]

        def send_sums(k):
            target = (px * ny + (py + k) % ny, om)
            push(sd.at[which, core, mu], sd.at[which, core, mu], SUM_Y + which, target)

        each(ny, send_sums)
        pending.append((sd.at[which, 0, pl.ds(0, ny - 1)], SUM_Y + which))

    def sums_x(which):
        arrive(sd.at[which, 0, pl.ds(0, ny - 1)], SUM_Y + which)

        def send_sums(k):
            target = ((px + k) % nx * ny + py, om)
            push(sd.at[which, core, group], sd.at[which, core, group], SUM_X + which, target)

        each(nx, send_sums)
        pending.append((sd.at[which, 0, pl.ds(0, (nx - 1) * ny)], SUM_X + which))

    def sums_core(which):
        arrive(sd.at[which, 0, pl.ds(0, (nx - 1) * ny)], SUM_X + which)
        push(sd.at[which, core], sd.at[which, core], SUM_C + which, (mu, pair))
        pending.append((sd.at[which, 0], SUM_C + which))

    def sums_all(which):
        arrive(sd.at[which, 0], SUM_C + which)
        for side in range(2):
            for part in range(2):
                block = jnp.swapaxes(sd[which, side, part * rows : (part + 1) * rows], 0, 1)
                summed[part, :, side] = block
        return tuple(summed[part].reshape(size, size) for part in range(2))

    arrive(shared.at[pl.ds(0, nmode - 1)], FIRST)
    sums_z(0, jnp.sum(shared[...], axis=0))
    arrive(got.at[0, pl.ds(0, nmode - 1)], ENTRY)
    mix(0)
    sums_y(0)
    arrive(hb.at[:, pl.ds(0, nz - 1), 0], FIELD_Z)
    push(hb.at[:, :, core], hb.at[:, :, core], FIELD_C, (mu, pair))
    pending.append((hb.at[:, :, 0], FIELD_C))
    arrive(got.at[1, pl.ds(0, nmode - 1)], ENTRY + 1)
    mix(1)
    sums_x(0)
    weights = jnp.concatenate(
        [abuf[0, :, :, modes:][:, None], abuf[1, :, :, modes:][:, None]], 1
    ).reshape(modes, LANES)
    wide = weights[:, :cols]
    own = prop[pl.ds(om, 1), :]
    sums_z(1, jnp.concatenate(
        [jnp.sum(wide * mixed[h], axis=0, keepdims=True) for h in range(2)], 1
    ))

    def spread(h):
        arrive(back.at[h, pl.ds(0, nmode - 1)], MIXED + h)
        stage2[h] = jnp.swapaxes(back[h], 0, 1).reshape(norb, 2, rows, cols)

        def send_matrix(k):
            target = (om + k) % norb
            push(stage2.at[h, target], whole.at[h, :, om], WHOLE + h, (mu, target))

        each(norb, send_matrix)
        whole[h, :, om] = stage2[h, om]
        pending.append((whole.at[h, :, pl.ds(0, norb - 1)], WHOLE + h))

    column = jnp.sum(weights[:, :1] * (ah[...].astype(F32) + al[...].astype(F32)), axis=0, keepdims=True)
    both = jnp.concatenate([own, column, jnp.zeros((6, modes), F32)], 0)
    products = jnp.dot(both, weights, precision=lax.Precision.HIGHEST, preferred_element_type=F32)
    e_own = products[0:1, 0:1]
    f_all = products[1:2, 0:1]
    c_all = jnp.sum(weights * weights, axis=0, keepdims=True)[:, :1]
    c_own = coup[om]
    arrive(hb.at[:, :, 0], FIELD_C)
    store_h(0, matrix(0), matrix(1))

    spread(0)
    sums_core(0)
    sums_y(1)

    source = sums_all(0)
    densities = [(matrix(2), matrix(3))]
    fields = tuple(matrix(part) for part in range(2))
    for step in range(2):
        source = turn(step, *source)
        source = tuple(source[p] + (c_all * time_step) * densities[step][p] for p in range(2))
        densities.append(tuple(densities[step][p] + time_step * source[p] for p in range(2)))
        fields = tuple(fields[p] + (field_weight * time_step) * source[p] for p in range(2))
        store_h(step + 1, *fields)

    spread(1)
    sums_x(1)
    for h in range(2):
        arrive(whole.at[h, :, pl.ds(0, norb - 1)], WHOLE + h)
    state = tuple(
        jnp.concatenate([whole[h, part].reshape(size, cols) for h in range(2)], 1)
        for part in range(2)
    )
    for step in range(3):
        weight = e_own if step < 2 else c_own
        state = turn(step, *state)
        state = tuple(state[p] + (weight * time_step) * densities[step][p] for p in range(2))
    for part in range(2):
        final[part] = state[part].reshape(norb, rows, size)

    def send_result(k):
        target = (om + k) % norb
        push(final.at[:, target], out.at[om], RESULT, (mu, target))

    each(norb, send_result)
    pending.append((out.at[pl.ds(0, norb - 1)], RESULT))
    out[om] = final[:, om]

    sums_core(1)
    chain = sums_all(1)
    for step in range(3):
        weight = f_all if step < 2 else c_all
        chain = turn(step, *chain)
        chain = tuple(chain[p] + (weight * time_step) * densities[step][p] for p in range(2))
    for part in range(2):
        summed[part] = (densities[2][part] + time_step * chain[part]).reshape(nz, CORES, rows, size)
    for part in range(2):
        dout[part] = summed[part, pz, core]

    arrive(out.at[pl.ds(0, norb - 1)], RESULT)
    for ref, index in pending:
        wait_for(ref, send.at[index])


def build(mesh, nx, ny):
    def on_device(correlators, density, bare_hamiltonian, coupling, propagator):
        local, _, rows, size = correlators.shape
        nmode, norb = mesh.shape["mode"], mesh.shape["orb"]
        nz = norb // CORES
        modes = nmode * norb
        vmem = pl.BlockSpec(memory_space=pltpu.VMEM)
        whole = pl.BlockSpec(memory_space=pltpu.HBM)
        return pl.pallas_call(
            functools.partial(kernel, (nx, ny, nz, rows, size)),
            out_shape=(
                jax.ShapeDtypeStruct(correlators.shape, F32),
                jax.ShapeDtypeStruct(density.shape, F32),
            ),
            in_specs=[whole, whole, whole, pl.BlockSpec(memory_space=pltpu.SMEM), whole],
            out_specs=(vmem, vmem),
            scratch_shapes=[
                pltpu.VMEM((local, 2 * rows, size), F32),
                pltpu.VMEM(density.shape, F32),
                pltpu.VMEM(density.shape, F32),
                pltpu.VMEM(propagator.shape, F32),
                pltpu.VMEM((2, nmode, norb, size // 2), F32),
                pltpu.VMEM((2, nmode, norb, size // 2), F32),
                pltpu.VMEM((2, nmode, norb // 2, modes + LANES), F32),
                pltpu.VMEM((modes, modes), BF16),
                pltpu.VMEM((modes, modes), BF16),
                pltpu.VMEM((4, nz, CORES, rows, size), F32),
                pltpu.VMEM((2, nz, 1, size), F32),
                pltpu.VMEM((nmode, 1, size), F32),
                pltpu.VMEM((nmode, 1, size), F32),
                pltpu.VMEM((2, 2, nmode, nz, size), F32),
                pltpu.VMEM((2, modes, size // 2), F32),
                pltpu.VMEM((2, nmode, norb, size // 2), F32),
                pltpu.VMEM((2, norb, 2, rows, size // 2), F32),
                pltpu.VMEM((2, 2, norb, rows, size // 2), F32),
                pltpu.VMEM((2, norb, rows, size), F32),
                pltpu.VMEM((2, nz, CORES, rows, size), F32),
                pltpu.VMEM((3, 2, 2 * size, 2 * size), BF16),
                pltpu.VMEM((3, 2, 2 * size, 2 * size), BF16),
                pltpu.SemaphoreType.DMA((2 * nx + 18,)),
                pltpu.SemaphoreType.DMA((2 * nx + 18,)),
                pltpu.SemaphoreType.DMA((4,)),
            ],
            compiler_params=pltpu.CompilerParams(
                collective_id=0, has_side_effects=True, vmem_limit_bytes=60 * 1024 * 1024
            ),
        )(
            correlators.reshape(local, 2 * rows, size),
            density, bare_hamiltonian, coupling, propagator,
        )

    in_specs = (
        P("mode", None, "orb", None),
        P(None, "orb", None),
        P(None, "orb", None),
        P("mode"),
        P("mode", None),
    )
    out_specs = (P("mode", None, "orb", None), P(None, "orb", None))
    return jax.shard_map(
        on_device, mesh=mesh, in_specs=in_specs, out_specs=out_specs, check_vma=False
    )


def solution(mesh):
    return build(mesh, 4, mesh.shape["mode"] // 4)
```

```python
import functools

import jax
import jax.numpy as jnp
from jax import lax
from jax.experimental import pallas as pl
from jax.experimental.pallas import tpu as pltpu
from jax.sharding import PartitionSpec as P

MESH = pl.DeviceIdType.MESH
time_step = 0.1
field_weight = 0.0625
LANES = 128
CORES = 2
F32 = jnp.float32
BF16 = jnp.bfloat16


def split(value):
    high = value.astype(BF16)
    return high, (value - high.astype(F32)).astype(BF16)


def dot(first, second):
    return jnp.dot(first, second, preferred_element_type=F32)


def dot3(first, second):
    return dot(first[0], second[0]) + (dot(first[0], second[1]) + dot(first[1], second[0]))


def wait_for(ref, sem):
    pltpu.make_async_copy(ref, ref, sem).wait()


def kernel(
    dims,
    gin_hbm, dens_hbm, bare_hbm, coup, prop_hbm,
    out, dout,
    gin, dens, bare, prop, stage, got, abuf, ah, al, hb, zbuf, shares, shared, sd, mixed, back, stage2, whole, final, summed, hl, hr,
    send, recv, load,
):
    nx, ny, nz, rows, size = dims
    nmode, norb = nx * ny, nz * CORES
    modes = nmode * norb
    half = norb // 2
    cols = size // 2
    PROP_Y, PROP_X, PROP_C = 0, 0, nx
    base = 2 * nx
    ENTRY, MIXED, WHOLE = base, base + 2, base + 4
    FIELD_Z, FIELD_C, RESULT, FIRST = base + 6, base + 7, base + 8, base + 9
    SUM_Z, SUM_Y, SUM_X, SUM_C = base + 10, base + 12, base + 14, base + 16
    NEAR_MIXED, NEAR_WHOLE = base + 18, base + 19
    mu, om = lax.axis_index("mode"), lax.axis_index("orb")
    px, py = mu // ny, mu % ny
    pz, core = om // CORES, om % CORES
    other = 1 - core
    pair = pz * CORES + other

    def push(src, dst, index, target):
        pltpu.make_async_remote_copy(
            src_ref=src, dst_ref=dst, send_sem=send.at[index], recv_sem=recv.at[index],
            device_id=target, device_id_type=MESH,
        ).start()

    pending = []

    def arrive(ref, index):
        wait_for(ref, recv.at[index])

    def each(count, body):
        def step(k, carry):
            body(k)
            return carry
        lax.fori_loop(1, count, step, 0)

    loads = [
        pltpu.make_async_copy(src, dst, load.at[i])
        for i, (src, dst) in enumerate(
            ((prop_hbm, prop), (gin_hbm, gin), (bare_hbm, bare), (dens_hbm, dens))
        )
    ]
    for copy in loads:
        copy.start()

    barrier = pltpu.get_barrier_semaphore()

    def greet_mode(k):
        pl.semaphore_signal(barrier, inc=1, device_id=((mu + k) % nmode, om), device_id_type=MESH)

    def greet_orb(k):
        pl.semaphore_signal(barrier, inc=1, device_id=(mu, (om + k) % norb), device_id_type=MESH)

    each(nmode, greet_mode)
    each(norb, greet_orb)

    loads[0].wait()
    abuf[core, mu] = prop[pl.ds(pl.multiple_of(core * half, half), half), :]
    pl.semaphore_wait(barrier, nmode + norb - 2)

    def send_prop_y(k):
        push(abuf.at[core, mu], abuf.at[core, mu], PROP_Y, (px * ny + (py + k) % ny, om))

    each(ny, send_prop_y)
    pending.append((abuf.at[0, pl.ds(0, ny - 1)], PROP_Y))

    def send_entries(h, k):
        nu = (mu + k) % nmode
        push(stage.at[h, nu], got.at[h, mu], ENTRY + h, (nu, om))

    def send_fields(k):
        target = (pz + k) % nz
        push(hb.at[:, pz, core], hb.at[:, pz, core], FIELD_Z, (mu, target * CORES + core))

    loads[1].wait()
    for h in range(2):
        stage[h] = jnp.swapaxes(gin[:, :, h * cols : (h + 1) * cols], 0, 1)
        if h == 0:
            each(nmode, functools.partial(send_entries, 0))
    pending.append((got.at[0, pl.ds(0, nmode - 1)], ENTRY))

    def span_of(d):
        return pl.ds(pl.multiple_of((px - d + nx) % nx * ny, ny), ny)

    near = om // half
    sides = (1 - near, near)
    order = [0, 1] + list(range(nx - 1, 1, -1))
    group = span_of(0)

    def cross(d):
        push(abuf.at[core, span_of(d)], abuf.at[core, span_of(d)], PROP_C + d, (mu, pair))
        pending.append((abuf.at[0, pl.ds(0, ny)], PROP_C + d))

    arrive(abuf.at[0, pl.ds(0, ny - 1)], PROP_Y)
    for d in order[1:]:
        push(abuf.at[core, group], abuf.at[core, group], PROP_X + d, ((px + d) % nx * ny + py, om))
        pending.append((abuf.at[0, pl.ds(0, ny)], PROP_X + d))
    cross(0)
    each(nmode, functools.partial(send_entries, 1))
    pending.append((got.at[1, pl.ds(0, nmode - 1)], ENTRY + 1))

    share = coup[0] * gin[0]
    for i in range(1, norb):
        share = share + coup[i] * gin[i]
    lanes = lax.broadcasted_iota(jnp.int32, (nmode, LANES), 1)
    line = jnp.zeros((nmode, LANES), F32)
    for i in range(norb):
        line = jnp.where(lanes == i, coup[i], line)
    shares[...] = jnp.concatenate([share, line], 1)[:, None, :]

    def send_share(k):
        nu = (mu + k) % nmode
        push(shares.at[nu], shared.at[mu], FIRST, (nu, om))

    each(nmode, send_share)
    pending.append((shared.at[pl.ds(0, nmode - 1)], FIRST))
    loads[2].wait()
    loads[3].wait()
    for part in range(2):
        hb[part, pz, core] = bare[part] + field_weight * dens[part]
        hb[2 + part, pz, core] = dens[part]
    each(nz, send_fields)
    pending.append((hb.at[:, pl.ds(0, nz - 1), 0], FIELD_Z))
    shared[mu] = shares[mu]
    for h in range(2):
        got[h, mu] = stage[h, mu]
    for d in order[1:]:
        arrive(abuf.at[0, pl.ds(0, ny)], PROP_X + d)
        cross(d)

    def matrix(part):
        return hb[part].reshape(size, size)

    def store_h(step, real, imag):
        rh, rl = split(time_step * real)
        ih, il = split(time_step * imag)
        for level, (r, i) in enumerate(((rh, ih), (rl, il))):
            hl[step, level, :size, :size] = r
            hl[step, level, size:, size:] = r
            hl[step, level, :size, size:] = -i
            hl[step, level, size:, :size] = i
            hr[step, level, :size, :size] = r
            hr[step, level, size:, size:] = r
            hr[step, level, :size, size:] = i
            hr[step, level, size:, :size] = -i

    def turn(step, real, imag):
        rh, rl = split(real)
        ih, il = split(imag)
        left = dot3(
            (hl[step, 0], hl[step, 1]),
            (jnp.concatenate([rh, ih], 0), jnp.concatenate([rl, il], 0)),
        )
        right = dot3(
            (jnp.concatenate([rh, ih], 1), jnp.concatenate([rl, il], 1)),
            (hr[step, 0], hr[step, 1]),
        )
        return (
            real + (left[size:] - right[:, size:]),
            imag - (left[:size] - right[:, :size]),
        )

    def unpack(d):
        arrive(abuf.at[0, pl.ds(0, ny)], PROP_C + d)

        def step(j, carry):
            k = (px - d + nx) % nx * ny + j
            block = jnp.concatenate([abuf[0, k], abuf[1, k]], 0)
            high, low = split(block)
            where = pl.ds(pl.multiple_of(k * norb, norb), norb)
            ah[where, :] = high
            al[where, :] = low
            return carry

        lax.fori_loop(0, ny, step, 0)

    def mix(h):
        high, low = split(got[h].reshape(modes, cols))
        span = ny * norb
        for d in order:
            if h == 0:
                unpack(d)
            first = (px - d + nx) % nx
            where = pl.ds(pl.multiple_of(first * span, span), span)
            mixed[h, where, :] = dot3((ah[where, :], al[where, :]), (high, low))

            if h:
                continue

            def send_mixed(k, first=first):
                nu = first * ny + (py + k) % ny
                rows_of = pl.ds(pl.multiple_of(nu * norb, norb), norb)
                push(mixed.at[h, rows_of], back.at[h, mu], MIXED, (nu, om))

            if d:
                send_mixed(0)
            each(ny, send_mixed)
        for side in range(2 * h):
            start = sides[side] * half

            def send_part(k):
                nu = (mu + k) % nmode
                rows_of = pl.ds(pl.multiple_of(nu * norb + start, half), half)
                there = back.at[h, mu, pl.ds(pl.multiple_of(start, half), half)]
                push(mixed.at[h, rows_of], there, (MIXED + 1, NEAR_MIXED)[side], (nu, om))

            each(nmode, send_part)
            pending.append((back.at[h, pl.ds(0, nmode - 1), pl.ds(0, half)], (MIXED + 1, NEAR_MIXED)[side]))
        back[h, mu] = mixed[h, pl.ds(pl.multiple_of(mu * norb, norb), norb), :]
        if h == 0:
            pending.append((back.at[h, pl.ds(0, nmode - 1)], MIXED))

    def sums_z(which, row):
        zbuf[which, pz] = row

        def send_sums(k):
            target = (mu, (pz + k) % nz * CORES + core)
            push(zbuf.at[which, pz], zbuf.at[which, pz], SUM_Z + which, target)

        each(nz, send_sums)
        pending.append((zbuf.at[which, pl.ds(0, nz - 1)], SUM_Z + which))

    def sums_y(which):
        arrive(zbuf.at[which, pl.ds(0, nz - 1)], SUM_Z + which)
        sd[which, core, mu] = zbuf[which][:, 0, :]

        def send_sums(k):
            target = (px * ny + (py + k) % ny, om)
            push(sd.at[which, core, mu], sd.at[which, core, mu], SUM_Y + which, target)

        each(ny, send_sums)
        pending.append((sd.at[which, 0, pl.ds(0, ny - 1)], SUM_Y + which))

    def sums_x(which):
        arrive(sd.at[which, 0, pl.ds(0, ny - 1)], SUM_Y + which)

        def send_sums(k):
            target = ((px + k) % nx * ny + py, om)
            push(sd.at[which, core, group], sd.at[which, core, group], SUM_X + which, target)

        each(nx, send_sums)
        pending.append((sd.at[which, 0, pl.ds(0, (nx - 1) * ny)], SUM_X + which))

    def sums_core(which):
        arrive(sd.at[which, 0, pl.ds(0, (nx - 1) * ny)], SUM_X + which)
        push(sd.at[which, core], sd.at[which, core], SUM_C + which, (mu, pair))
        pending.append((sd.at[which, 0], SUM_C + which))

    def sums_all(which):
        arrive(sd.at[which, 0], SUM_C + which)
        for side in range(2):
            for part in range(2):
                block = jnp.swapaxes(sd[which, side, part * rows : (part + 1) * rows], 0, 1)
                summed[part, :, side] = block
        return tuple(summed[part].reshape(size, size) for part in range(2))

    arrive(shared.at[pl.ds(0, nmode - 1)], FIRST)
    sums_z(0, jnp.sum(shared[:, :, :size], axis=0))
    arrive(got.at[0, pl.ds(0, nmode - 1)], ENTRY)
    mix(0)
    sums_y(0)
    arrive(hb.at[:, pl.ds(0, nz - 1), 0], FIELD_Z)
    push(hb.at[:, :, core], hb.at[:, :, core], FIELD_C, (mu, pair))
    pending.append((hb.at[:, :, 0], FIELD_C))
    arrive(got.at[1, pl.ds(0, nmode - 1)], ENTRY + 1)
    mix(1)
    sums_x(0)
    tall = jnp.broadcast_to(shared[:, :, size:], (nmode, norb, LANES)).reshape(modes, LANES)
    at_lane = lax.broadcasted_iota(jnp.int32, (modes, LANES), 1)
    at_row = lax.broadcasted_iota(jnp.int32, (modes, LANES), 0)
    weights = jnp.dot(
        jnp.where(at_lane == at_row % norb, tall, 0.0), jnp.ones((LANES, LANES), F32),
        precision=lax.Precision.HIGHEST, preferred_element_type=F32,
    )
    wide = weights[:, :cols]
    own = prop[pl.ds(om, 1), :]
    sums_z(1, jnp.concatenate(
        [jnp.sum(wide * mixed[h], axis=0, keepdims=True) for h in range(2)], 1
    ))

    def spread(h):
        arrive(back.at[h, pl.ds(0, nmode - 1)], MIXED + h)
        stage2[h] = jnp.swapaxes(back[h], 0, 1).reshape(norb, 2, rows, cols)

        def send_matrix(k):
            target = (om + k) % norb
            push(stage2.at[h, target], whole.at[h, :, om], WHOLE + h, (mu, target))

        each(norb, send_matrix)
        whole[h, :, om] = stage2[h, om]
        pending.append((whole.at[h, :, pl.ds(0, norb - 1)], WHOLE + h))

    def spread_side(side):
        arrive(back.at[1, pl.ds(0, nmode - 1), pl.ds(0, half)], (MIXED + 1, NEAR_MIXED)[side])
        start = pl.multiple_of(sides[side] * half, half)
        block = jnp.swapaxes(back[1, :, pl.ds(start, half), :], 0, 1)
        stage2[1, pl.ds(start, half)] = block.reshape(half, 2, rows, cols)
        index = (WHOLE + 1, NEAR_WHOLE)[side]

        def send_matrix(k):
            target = start + (om + k) % half
            push(stage2.at[1, target], whole.at[1, :, om], index, (mu, target))

        if side == 0:
            send_matrix(0)
        each(half, send_matrix)
        count = half - side
        pending.append((whole.at[1, :, pl.ds(0, count)], index))
        if side:
            whole[1, :, om] = stage2[1, om]

    column = jnp.sum(weights[:, :1] * (ah[...].astype(F32) + al[...].astype(F32)), axis=0, keepdims=True)
    both = jnp.concatenate([own, column, jnp.zeros((6, modes), F32)], 0)
    products = jnp.dot(both, weights, precision=lax.Precision.HIGHEST, preferred_element_type=F32)
    e_own = products[0:1, 0:1]
    f_all = products[1:2, 0:1]
    c_all = jnp.sum(weights * weights, axis=0, keepdims=True)[:, :1]
    c_own = coup[om]
    arrive(hb.at[:, :, 0], FIELD_C)
    store_h(0, matrix(0), matrix(1))

    spread(0)
    sums_core(0)
    sums_y(1)

    spread_side(0)
    spread_side(1)
    sums_x(1)

    source = sums_all(0)
    densities = [(matrix(2), matrix(3))]
    fields = tuple(matrix(part) for part in range(2))
    for step in range(2):
        source = turn(step, *source)
        source = tuple(source[p] + (c_all * time_step) * densities[step][p] for p in range(2))
        densities.append(tuple(densities[step][p] + time_step * source[p] for p in range(2)))
        fields = tuple(fields[p] + (field_weight * time_step) * source[p] for p in range(2))
        store_h(step + 1, *fields)

    arrive(whole.at[0, :, pl.ds(0, norb - 1)], WHOLE)
    arrive(whole.at[1, :, pl.ds(0, half)], WHOLE + 1)
    arrive(whole.at[1, :, pl.ds(0, half - 1)], NEAR_WHOLE)
    state = tuple(
        jnp.concatenate([whole[h, part].reshape(size, cols) for h in range(2)], 1)
        for part in range(2)
    )
    for step in range(3):
        weight = e_own if step < 2 else c_own
        state = turn(step, *state)
        state = tuple(state[p] + (weight * time_step) * densities[step][p] for p in range(2))
    for part in range(2):
        final[part] = state[part].reshape(norb, rows, size)

    def send_result(k):
        target = (om + k) % norb
        push(final.at[:, target], out.at[om], RESULT, (mu, target))

    each(norb, send_result)
    pending.append((out.at[pl.ds(0, norb - 1)], RESULT))
    out[om] = final[:, om]

    sums_core(1)
    chain = sums_all(1)
    for step in range(3):
        weight = f_all if step < 2 else c_all
        chain = turn(step, *chain)
        chain = tuple(chain[p] + (weight * time_step) * densities[step][p] for p in range(2))
    for part in range(2):
        summed[part] = (densities[2][part] + time_step * chain[part]).reshape(nz, CORES, rows, size)
    for part in range(2):
        dout[part] = summed[part, pz, core]

    arrive(out.at[pl.ds(0, norb - 1)], RESULT)
    for ref, index in pending:
        wait_for(ref, send.at[index])


def build(mesh, nx, ny):
    def on_device(correlators, density, bare_hamiltonian, coupling, propagator):
        local, _, rows, size = correlators.shape
        nmode, norb = mesh.shape["mode"], mesh.shape["orb"]
        nz = norb // CORES
        modes = nmode * norb
        vmem = pl.BlockSpec(memory_space=pltpu.VMEM)
        whole = pl.BlockSpec(memory_space=pltpu.HBM)
        return pl.pallas_call(
            functools.partial(kernel, (nx, ny, nz, rows, size)),
            out_shape=(
                jax.ShapeDtypeStruct(correlators.shape, F32),
                jax.ShapeDtypeStruct(density.shape, F32),
            ),
            in_specs=[whole, whole, whole, pl.BlockSpec(memory_space=pltpu.SMEM), whole],
            out_specs=(vmem, vmem),
            scratch_shapes=[
                pltpu.VMEM((local, 2 * rows, size), F32),
                pltpu.VMEM(density.shape, F32),
                pltpu.VMEM(density.shape, F32),
                pltpu.VMEM(propagator.shape, F32),
                pltpu.VMEM((2, nmode, norb, size // 2), F32),
                pltpu.VMEM((2, nmode, norb, size // 2), F32),
                pltpu.VMEM((2, nmode, norb // 2, modes), F32),
                pltpu.VMEM((modes, modes), BF16),
                pltpu.VMEM((modes, modes), BF16),
                pltpu.VMEM((4, nz, CORES, rows, size), F32),
                pltpu.VMEM((2, nz, 1, size), F32),
                pltpu.VMEM((nmode, 1, size + LANES), F32),
                pltpu.VMEM((nmode, 1, size + LANES), F32),
                pltpu.VMEM((2, 2, nmode, nz, size), F32),
                pltpu.VMEM((2, modes, size // 2), F32),
                pltpu.VMEM((2, nmode, norb, size // 2), F32),
                pltpu.VMEM((2, norb, 2, rows, size // 2), F32),
                pltpu.VMEM((2, 2, norb, rows, size // 2), F32),
                pltpu.VMEM((2, norb, rows, size), F32),
                pltpu.VMEM((2, nz, CORES, rows, size), F32),
                pltpu.VMEM((3, 2, 2 * size, 2 * size), BF16),
                pltpu.VMEM((3, 2, 2 * size, 2 * size), BF16),
                pltpu.SemaphoreType.DMA((2 * nx + 20,)),
                pltpu.SemaphoreType.DMA((2 * nx + 20,)),
                pltpu.SemaphoreType.DMA((4,)),
            ],
            compiler_params=pltpu.CompilerParams(
                collective_id=0, has_side_effects=True, vmem_limit_bytes=60 * 1024 * 1024
            ),
        )(
            correlators.reshape(local, 2 * rows, size),
            density, bare_hamiltonian, coupling, propagator,
        )

    in_specs = (
        P("mode", None, "orb", None),
        P(None, "orb", None),
        P(None, "orb", None),
        P("mode"),
        P("mode", None),
    )
    out_specs = (P("mode", None, "orb", None), P(None, "orb", None))
    return jax.shard_map(
        on_device, mesh=mesh, in_specs=in_specs, out_specs=out_specs, check_vma=False
    )


def solution(mesh):
    return build(mesh, 4, mesh.shape["mode"] // 4)
```

```python
import functools

import jax
import jax.numpy as jnp
from jax import lax
from jax.experimental import pallas as pl
from jax.experimental.pallas import tpu as pltpu
from jax.sharding import PartitionSpec as P

MESH = pl.DeviceIdType.MESH
time_step = 0.1
field_weight = 0.0625
LANES = 128
CORES = 2
F32 = jnp.float32
BF16 = jnp.bfloat16


def split(value):
    high = value.astype(BF16)
    return high, (value - high.astype(F32)).astype(BF16)


def dot(first, second):
    return jnp.dot(first, second, preferred_element_type=F32)


def dot3(first, second):
    return dot(first[0], second[0]) + (dot(first[0], second[1]) + dot(first[1], second[0]))


def wait_for(ref, sem):
    pltpu.make_async_copy(ref, ref, sem).wait()


def kernel(
    dims,
    gin_hbm, dens_hbm, bare_hbm, coup, prop_hbm,
    out, dout,
    gin, dens, bare, prop, stage, got, abuf, ah, al, hb, zbuf, shares, shared, sd, mixed, back, stage2, whole, final, summed, hl, hr,
    send, recv, load,
):
    nx, ny, nz, rows, size = dims
    nmode, norb = nx * ny, nz * CORES
    modes = nmode * norb
    half = norb // 2
    cols = size // 2
    PROP_Y, PROP_X, PROP_C = 0, 0, nx
    base = 2 * nx
    ENTRY, MIXED, WHOLE = base, base + 2, base + 4
    FIELD_Z, FIELD_C, RESULT, FIRST = base + 6, base + 7, base + 8, base + 9
    SUM_Z, SUM_Y, SUM_X, SUM_C = base + 10, base + 12, base + 14, base + 16
    NEAR_MIXED, NEAR_WHOLE = base + 18, base + 19
    mu, om = lax.axis_index("mode"), lax.axis_index("orb")
    px, py = mu // ny, mu % ny
    pz, core = om // CORES, om % CORES
    other = 1 - core
    pair = pz * CORES + other

    def push(src, dst, index, target):
        pltpu.make_async_remote_copy(
            src_ref=src, dst_ref=dst, send_sem=send.at[index], recv_sem=recv.at[index],
            device_id=target, device_id_type=MESH,
        ).start()

    pending = []

    def arrive(ref, index):
        wait_for(ref, recv.at[index])

    def each(count, body):
        def step(k, carry):
            body(k)
            return carry
        lax.fori_loop(1, count, step, 0)

    loads = [
        pltpu.make_async_copy(src, dst, load.at[i])
        for i, (src, dst) in enumerate(
            ((prop_hbm, prop), (gin_hbm, gin), (bare_hbm, bare), (dens_hbm, dens))
        )
    ]
    for copy in loads:
        copy.start()

    barrier = pltpu.get_barrier_semaphore()

    def greet_mode(k):
        pl.semaphore_signal(barrier, inc=1, device_id=((mu + k) % nmode, om), device_id_type=MESH)

    def greet_orb(k):
        pl.semaphore_signal(barrier, inc=1, device_id=(mu, (om + k) % norb), device_id_type=MESH)

    each(nmode, greet_mode)
    each(norb, greet_orb)

    loads[0].wait()
    abuf[core, mu] = prop[pl.ds(pl.multiple_of(core * half, half), half), :]
    pl.semaphore_wait(barrier, nmode + norb - 2)

    def send_prop_y(k):
        push(abuf.at[core, mu], abuf.at[core, mu], PROP_Y, (px * ny + (py + k) % ny, om))

    each(ny, send_prop_y)
    pending.append((abuf.at[0, pl.ds(0, ny - 1)], PROP_Y))

    def send_entries(h, k):
        nu = (mu + k) % nmode
        push(stage.at[h, nu], got.at[h, mu], ENTRY + h, (nu, om))

    def send_fields(k):
        target = (pz + k) % nz
        push(hb.at[:, pz, core], hb.at[:, pz, core], FIELD_Z, (mu, target * CORES + core))

    loads[1].wait()
    share = coup[0] * gin[0]
    for i in range(1, norb):
        share = share + coup[i] * gin[i]
    lanes = lax.broadcasted_iota(jnp.int32, (nmode, LANES), 1)
    line = jnp.zeros((nmode, LANES), F32)
    for i in range(norb):
        line = jnp.where(lanes == i, coup[i], line)
    shares[...] = jnp.concatenate([share, line], 1)[:, None, :]

    def send_share(k):
        nu = (mu + k) % nmode
        push(shares.at[nu], shared.at[mu], FIRST, (nu, om))

    each(nmode, send_share)
    pending.append((shared.at[pl.ds(0, nmode - 1)], FIRST))
    shared[mu] = shares[mu]
    for h in range(2):
        stage[h] = jnp.swapaxes(gin[:, :, h * cols : (h + 1) * cols], 0, 1)
        if h == 0:
            each(nmode, functools.partial(send_entries, 0))
    pending.append((got.at[0, pl.ds(0, nmode - 1)], ENTRY))

    def span_of(d):
        return pl.ds(pl.multiple_of((px - d + nx) % nx * ny, ny), ny)

    near = om // half
    sides = (1 - near, near)
    order = [0, 1] + list(range(nx - 1, 1, -1))
    group = span_of(0)

    def cross(d):
        push(abuf.at[core, span_of(d)], abuf.at[core, span_of(d)], PROP_C + d, (mu, pair))
        pending.append((abuf.at[0, pl.ds(0, ny)], PROP_C + d))

    arrive(abuf.at[0, pl.ds(0, ny - 1)], PROP_Y)
    for d in order[1:]:
        push(abuf.at[core, group], abuf.at[core, group], PROP_X + d, ((px + d) % nx * ny + py, om))
        pending.append((abuf.at[0, pl.ds(0, ny)], PROP_X + d))
    cross(0)
    each(nmode, functools.partial(send_entries, 1))
    pending.append((got.at[1, pl.ds(0, nmode - 1)], ENTRY + 1))

    loads[2].wait()
    loads[3].wait()
    for part in range(2):
        hb[part, pz, core] = bare[part] + field_weight * dens[part]
        hb[2 + part, pz, core] = dens[part]
    each(nz, send_fields)
    pending.append((hb.at[:, pl.ds(0, nz - 1), 0], FIELD_Z))
    for h in range(2):
        got[h, mu] = stage[h, mu]

    def sums_z(which, row):
        zbuf[which, pz] = row

        def send_sums(k):
            target = (mu, (pz + k) % nz * CORES + core)
            push(zbuf.at[which, pz], zbuf.at[which, pz], SUM_Z + which, target)

        each(nz, send_sums)
        pending.append((zbuf.at[which, pl.ds(0, nz - 1)], SUM_Z + which))

    def sums_y(which):
        arrive(zbuf.at[which, pl.ds(0, nz - 1)], SUM_Z + which)
        sd[which, core, mu] = zbuf[which][:, 0, :]

        def send_sums(k):
            target = (px * ny + (py + k) % ny, om)
            push(sd.at[which, core, mu], sd.at[which, core, mu], SUM_Y + which, target)

        each(ny, send_sums)
        pending.append((sd.at[which, 0, pl.ds(0, ny - 1)], SUM_Y + which))

    def sums_x(which):
        arrive(sd.at[which, 0, pl.ds(0, ny - 1)], SUM_Y + which)

        def send_sums(k):
            target = ((px + k) % nx * ny + py, om)
            push(sd.at[which, core, group], sd.at[which, core, group], SUM_X + which, target)

        each(nx, send_sums)
        pending.append((sd.at[which, 0, pl.ds(0, (nx - 1) * ny)], SUM_X + which))

    def sums_core(which):
        arrive(sd.at[which, 0, pl.ds(0, (nx - 1) * ny)], SUM_X + which)
        push(sd.at[which, core], sd.at[which, core], SUM_C + which, (mu, pair))
        pending.append((sd.at[which, 0], SUM_C + which))

    def sums_all(which):
        arrive(sd.at[which, 0], SUM_C + which)
        for side in range(2):
            for part in range(2):
                block = jnp.swapaxes(sd[which, side, part * rows : (part + 1) * rows], 0, 1)
                summed[part, :, side] = block
        return tuple(summed[part].reshape(size, size) for part in range(2))

    arrive(shared.at[pl.ds(0, nmode - 1)], FIRST)
    sums_z(0, jnp.sum(shared[:, :, :size], axis=0))
    for d in order[1:]:
        arrive(abuf.at[0, pl.ds(0, ny)], PROP_X + d)
        cross(d)
    sums_y(0)

    def matrix(part):
        return hb[part].reshape(size, size)

    def store_h(step, real, imag):
        rh, rl = split(time_step * real)
        ih, il = split(time_step * imag)
        for level, (r, i) in enumerate(((rh, ih), (rl, il))):
            hl[step, level, :size, :size] = r
            hl[step, level, size:, size:] = r
            hl[step, level, :size, size:] = -i
            hl[step, level, size:, :size] = i
            hr[step, level, :size, :size] = r
            hr[step, level, size:, size:] = r
            hr[step, level, :size, size:] = i
            hr[step, level, size:, :size] = -i

    def turn(step, real, imag):
        rh, rl = split(real)
        ih, il = split(imag)
        left = dot3(
            (hl[step, 0], hl[step, 1]),
            (jnp.concatenate([rh, ih], 0), jnp.concatenate([rl, il], 0)),
        )
        right = dot3(
            (jnp.concatenate([rh, ih], 1), jnp.concatenate([rl, il], 1)),
            (hr[step, 0], hr[step, 1]),
        )
        return (
            real + (left[size:] - right[:, size:]),
            imag - (left[:size] - right[:, :size]),
        )

    def unpack(d):
        arrive(abuf.at[0, pl.ds(0, ny)], PROP_C + d)

        def step(j, carry):
            k = (px - d + nx) % nx * ny + j
            block = jnp.concatenate([abuf[0, k], abuf[1, k]], 0)
            high, low = split(block)
            where = pl.ds(pl.multiple_of(k * norb, norb), norb)
            ah[where, :] = high
            al[where, :] = low
            return carry

        lax.fori_loop(0, ny, step, 0)

    def mix(h):
        high, low = split(got[h].reshape(modes, cols))
        span = ny * norb
        for d in order:
            if h == 0:
                unpack(d)
            first = (px - d + nx) % nx
            where = pl.ds(pl.multiple_of(first * span, span), span)
            mixed[h, where, :] = dot3((ah[where, :], al[where, :]), (high, low))

            if h:
                continue

            def send_mixed(k, first=first):
                nu = first * ny + (py + k) % ny
                rows_of = pl.ds(pl.multiple_of(nu * norb, norb), norb)
                push(mixed.at[h, rows_of], back.at[h, mu], MIXED, (nu, om))

            if d:
                send_mixed(0)
            each(ny, send_mixed)
        for side in range(2 * h):
            start = sides[side] * half

            def send_part(k):
                nu = (mu + k) % nmode
                rows_of = pl.ds(pl.multiple_of(nu * norb + start, half), half)
                there = back.at[h, mu, pl.ds(pl.multiple_of(start, half), half)]
                push(mixed.at[h, rows_of], there, (MIXED + 1, NEAR_MIXED)[side], (nu, om))

            each(nmode, send_part)
            pending.append((back.at[h, pl.ds(0, nmode - 1), pl.ds(0, half)], (MIXED + 1, NEAR_MIXED)[side]))
        back[h, mu] = mixed[h, pl.ds(pl.multiple_of(mu * norb, norb), norb), :]
        if h == 0:
            pending.append((back.at[h, pl.ds(0, nmode - 1)], MIXED))

    arrive(got.at[0, pl.ds(0, nmode - 1)], ENTRY)
    mix(0)
    arrive(hb.at[:, pl.ds(0, nz - 1), 0], FIELD_Z)
    push(hb.at[:, :, core], hb.at[:, :, core], FIELD_C, (mu, pair))
    pending.append((hb.at[:, :, 0], FIELD_C))
    arrive(got.at[1, pl.ds(0, nmode - 1)], ENTRY + 1)
    mix(1)
    sums_x(0)
    tall = jnp.broadcast_to(shared[:, :, size:], (nmode, norb, LANES)).reshape(modes, LANES)
    at_lane = lax.broadcasted_iota(jnp.int32, (modes, LANES), 1)
    at_row = lax.broadcasted_iota(jnp.int32, (modes, LANES), 0)
    weights = jnp.dot(
        jnp.where(at_lane == at_row % norb, tall, 0.0), jnp.ones((LANES, LANES), F32),
        precision=lax.Precision.HIGHEST, preferred_element_type=F32,
    )
    wide = weights[:, :cols]
    own = prop[pl.ds(om, 1), :]
    sums_z(1, jnp.concatenate(
        [jnp.sum(wide * mixed[h], axis=0, keepdims=True) for h in range(2)], 1
    ))

    def spread(h):
        arrive(back.at[h, pl.ds(0, nmode - 1)], MIXED + h)
        stage2[h] = jnp.swapaxes(back[h], 0, 1).reshape(norb, 2, rows, cols)

        def send_matrix(k):
            target = (om + k) % norb
            push(stage2.at[h, target], whole.at[h, :, om], WHOLE + h, (mu, target))

        each(norb, send_matrix)
        whole[h, :, om] = stage2[h, om]
        pending.append((whole.at[h, :, pl.ds(0, norb - 1)], WHOLE + h))

    def spread_side(side):
        arrive(back.at[1, pl.ds(0, nmode - 1), pl.ds(0, half)], (MIXED + 1, NEAR_MIXED)[side])
        start = pl.multiple_of(sides[side] * half, half)
        block = jnp.swapaxes(back[1, :, pl.ds(start, half), :], 0, 1)
        stage2[1, pl.ds(start, half)] = block.reshape(half, 2, rows, cols)
        index = (WHOLE + 1, NEAR_WHOLE)[side]

        def send_matrix(k):
            target = start + (om + k) % half
            push(stage2.at[1, target], whole.at[1, :, om], index, (mu, target))

        if side == 0:
            send_matrix(0)
        each(half, send_matrix)
        count = half - side
        pending.append((whole.at[1, :, pl.ds(0, count)], index))
        if side:
            whole[1, :, om] = stage2[1, om]

    spread(0)
    sums_core(0)

    column = jnp.sum(weights[:, :1] * (ah[...].astype(F32) + al[...].astype(F32)), axis=0, keepdims=True)
    both = jnp.concatenate([own, column, jnp.zeros((6, modes), F32)], 0)
    products = jnp.dot(both, weights, precision=lax.Precision.HIGHEST, preferred_element_type=F32)
    e_own = products[0:1, 0:1]
    f_all = products[1:2, 0:1]
    c_all = jnp.sum(weights * weights, axis=0, keepdims=True)[:, :1]
    c_own = coup[om]
    arrive(hb.at[:, :, 0], FIELD_C)
    store_h(0, matrix(0), matrix(1))


    spread_side(0)
    sums_y(1)
    spread_side(1)
    sums_x(1)
    source = sums_all(0)
    densities = [(matrix(2), matrix(3))]
    fields = tuple(matrix(part) for part in range(2))
    for step in range(2):
        source = turn(step, *source)
        source = tuple(source[p] + (c_all * time_step) * densities[step][p] for p in range(2))
        densities.append(tuple(densities[step][p] + time_step * source[p] for p in range(2)))
        fields = tuple(fields[p] + (field_weight * time_step) * source[p] for p in range(2))
        store_h(step + 1, *fields)

    arrive(whole.at[0, :, pl.ds(0, norb - 1)], WHOLE)
    arrive(whole.at[1, :, pl.ds(0, half)], WHOLE + 1)
    arrive(whole.at[1, :, pl.ds(0, half - 1)], NEAR_WHOLE)
    state = tuple(
        jnp.concatenate([whole[h, part].reshape(size, cols) for h in range(2)], 1)
        for part in range(2)
    )
    for step in range(3):
        weight = e_own if step < 2 else c_own
        state = turn(step, *state)
        state = tuple(state[p] + (weight * time_step) * densities[step][p] for p in range(2))
    for part in range(2):
        final[part] = state[part].reshape(norb, rows, size)

    def send_result(k):
        target = (om + k) % norb
        push(final.at[:, target], out.at[om], RESULT, (mu, target))

    each(norb, send_result)
    pending.append((out.at[pl.ds(0, norb - 1)], RESULT))
    keep = pltpu.make_async_copy(final.at[:, om], out.at[om], load.at[0])
    keep.start()

    sums_core(1)
    chain = sums_all(1)
    for step in range(3):
        weight = f_all if step < 2 else c_all
        chain = turn(step, *chain)
        chain = tuple(chain[p] + (weight * time_step) * densities[step][p] for p in range(2))
    for part in range(2):
        summed[part] = (densities[2][part] + time_step * chain[part]).reshape(nz, CORES, rows, size)
    for part in range(2):
        dout[part] = summed[part, pz, core]

    keep.wait()
    arrive(out.at[pl.ds(0, norb - 1)], RESULT)
    for ref, index in pending:
        wait_for(ref, send.at[index])


def build(mesh, nx, ny):
    def on_device(correlators, density, bare_hamiltonian, coupling, propagator):
        local, _, rows, size = correlators.shape
        nmode, norb = mesh.shape["mode"], mesh.shape["orb"]
        nz = norb // CORES
        modes = nmode * norb
        vmem = pl.BlockSpec(memory_space=pltpu.VMEM)
        whole = pl.BlockSpec(memory_space=pltpu.HBM)
        return pl.pallas_call(
            functools.partial(kernel, (nx, ny, nz, rows, size)),
            out_shape=(
                jax.ShapeDtypeStruct(correlators.shape, F32),
                jax.ShapeDtypeStruct(density.shape, F32),
            ),
            in_specs=[whole, whole, whole, pl.BlockSpec(memory_space=pltpu.SMEM), whole],
            out_specs=(whole, vmem),
            scratch_shapes=[
                pltpu.VMEM((local, 2 * rows, size), F32),
                pltpu.VMEM(density.shape, F32),
                pltpu.VMEM(density.shape, F32),
                pltpu.VMEM(propagator.shape, F32),
                pltpu.VMEM((2, nmode, norb, size // 2), F32),
                pltpu.VMEM((2, nmode, norb, size // 2), F32),
                pltpu.VMEM((2, nmode, norb // 2, modes), F32),
                pltpu.VMEM((modes, modes), BF16),
                pltpu.VMEM((modes, modes), BF16),
                pltpu.VMEM((4, nz, CORES, rows, size), F32),
                pltpu.VMEM((2, nz, 1, size), F32),
                pltpu.VMEM((nmode, 1, size + LANES), F32),
                pltpu.VMEM((nmode, 1, size + LANES), F32),
                pltpu.VMEM((2, 2, nmode, nz, size), F32),
                pltpu.VMEM((2, modes, size // 2), F32),
                pltpu.VMEM((2, nmode, norb, size // 2), F32),
                pltpu.VMEM((2, norb, 2, rows, size // 2), F32),
                pltpu.VMEM((2, 2, norb, rows, size // 2), F32),
                pltpu.VMEM((2, norb, rows, size), F32),
                pltpu.VMEM((2, nz, CORES, rows, size), F32),
                pltpu.VMEM((3, 2, 2 * size, 2 * size), BF16),
                pltpu.VMEM((3, 2, 2 * size, 2 * size), BF16),
                pltpu.SemaphoreType.DMA((2 * nx + 20,)),
                pltpu.SemaphoreType.DMA((2 * nx + 20,)),
                pltpu.SemaphoreType.DMA((4,)),
            ],
            compiler_params=pltpu.CompilerParams(
                collective_id=0, has_side_effects=True, vmem_limit_bytes=60 * 1024 * 1024
            ),
        )(
            correlators.reshape(local, 2 * rows, size),
            density, bare_hamiltonian, coupling, propagator,
        )

    in_specs = (
        P("mode", None, "orb", None),
        P(None, "orb", None),
        P(None, "orb", None),
        P("mode"),
        P("mode", None),
    )
    out_specs = (P("mode", None, "orb", None), P(None, "orb", None))
    return jax.shard_map(
        on_device, mesh=mesh, in_specs=in_specs, out_specs=out_specs, check_vma=False
    )


def solution(mesh):
    return build(mesh, 4, mesh.shape["mode"] // 4)
```

```python
import functools

import jax
import jax.numpy as jnp
from jax import lax
from jax.experimental import pallas as pl
from jax.experimental.pallas import tpu as pltpu
from jax.sharding import PartitionSpec as P

MESH = pl.DeviceIdType.MESH
time_step = 0.1
field_weight = 0.0625
LANES = 128
CORES = 2
F32 = jnp.float32
BF16 = jnp.bfloat16


def split(value):
    high = value.astype(BF16)
    return high, (value - high.astype(F32)).astype(BF16)


def dot(first, second):
    return jnp.dot(first, second, preferred_element_type=F32)


def dot3(first, second):
    return dot(first[0], second[0]) + (dot(first[0], second[1]) + dot(first[1], second[0]))


def wait_for(ref, sem):
    pltpu.make_async_copy(ref, ref, sem).wait()


def kernel(
    dims,
    gin_hbm, dens_hbm, bare_hbm, coup, prop_hbm,
    out, dout,
    gin, dens, bare, prop, stage, got, abuf, ah, al, hb, zbuf, shares, shared, sd, mixed, back, stage2, whole, final, summed, hl, hr,
    send, recv, load,
):
    nx, ny, nz, rows, size = dims
    nmode, norb = nx * ny, nz * CORES
    modes = nmode * norb
    half = norb // 2
    cols = size // 2
    PROP_Y, PROP_X, PROP_C = 0, 0, nx
    base = 2 * nx
    ENTRY, MIXED, WHOLE = base, base + 2, base + 4
    FIELD_Z, FIELD_C, RESULT, FIRST = base + 6, base + 7, base + 8, base + 9
    SUM_Z, SUM_Y, SUM_X, SUM_C = base + 10, base + 12, base + 14, base + 16
    NEAR_MIXED, NEAR_WHOLE = base + 18, base + 20
    mu, om = lax.axis_index("mode"), lax.axis_index("orb")
    px, py = mu // ny, mu % ny
    pz, core = om // CORES, om % CORES
    other = 1 - core
    pair = pz * CORES + other

    def push(src, dst, index, target):
        pltpu.make_async_remote_copy(
            src_ref=src, dst_ref=dst, send_sem=send.at[index], recv_sem=recv.at[index],
            device_id=target, device_id_type=MESH,
        ).start()

    pending = []

    def arrive(ref, index):
        wait_for(ref, recv.at[index])

    def each(count, body):
        def step(k, carry):
            body(k)
            return carry
        lax.fori_loop(1, count, step, 0)

    loads = [
        pltpu.make_async_copy(src, dst, load.at[i])
        for i, (src, dst) in enumerate(
            ((prop_hbm, prop), (gin_hbm, gin), (bare_hbm, bare), (dens_hbm, dens))
        )
    ]
    for copy in loads:
        copy.start()

    barrier = pltpu.get_barrier_semaphore()

    def greet_mode(k):
        pl.semaphore_signal(barrier, inc=1, device_id=((mu + k) % nmode, om), device_id_type=MESH)

    def greet_orb(k):
        pl.semaphore_signal(barrier, inc=1, device_id=(mu, (om + k) % norb), device_id_type=MESH)

    each(nmode, greet_mode)
    each(norb, greet_orb)

    loads[0].wait()
    abuf[core, mu] = prop[pl.ds(pl.multiple_of(core * half, half), half), :]
    pl.semaphore_wait(barrier, nmode + norb - 2)

    def send_prop_y(k):
        push(abuf.at[core, mu], abuf.at[core, mu], PROP_Y, (px * ny + (py + k) % ny, om))

    each(ny, send_prop_y)
    pending.append((abuf.at[0, pl.ds(0, ny - 1)], PROP_Y))

    def send_entries(h, k):
        nu = (mu + k) % nmode
        push(stage.at[h, nu], got.at[h, mu], ENTRY + h, (nu, om))

    def send_fields(k):
        target = (pz + k) % nz
        push(hb.at[:, pz, core], hb.at[:, pz, core], FIELD_Z, (mu, target * CORES + core))

    loads[1].wait()
    share = coup[0] * gin[0]
    for i in range(1, norb):
        share = share + coup[i] * gin[i]
    lanes = lax.broadcasted_iota(jnp.int32, (nmode, LANES), 1)
    line = jnp.zeros((nmode, LANES), F32)
    for i in range(norb):
        line = jnp.where(lanes == i, coup[i], line)
    shares[...] = jnp.concatenate([share, line], 1)[:, None, :]

    def send_share(k):
        nu = (mu + k) % nmode
        push(shares.at[nu], shared.at[mu], FIRST, (nu, om))

    each(nmode, send_share)
    pending.append((shared.at[pl.ds(0, nmode - 1)], FIRST))
    shared[mu] = shares[mu]
    for h in range(2):
        stage[h] = jnp.swapaxes(gin[:, :, h * cols : (h + 1) * cols], 0, 1)
        if h == 0:
            each(nmode, functools.partial(send_entries, 0))
    pending.append((got.at[0, pl.ds(0, nmode - 1)], ENTRY))

    def span_of(d):
        return pl.ds(pl.multiple_of((px - d + nx) % nx * ny, ny), ny)

    near = om // half
    sides = (1 - near, near)
    order = [0, 1] + list(range(nx - 1, 1, -1))
    group = span_of(0)

    def cross(d):
        push(abuf.at[core, span_of(d)], abuf.at[core, span_of(d)], PROP_C + d, (mu, pair))
        pending.append((abuf.at[0, pl.ds(0, ny)], PROP_C + d))

    arrive(abuf.at[0, pl.ds(0, ny - 1)], PROP_Y)
    for d in order[1:]:
        push(abuf.at[core, group], abuf.at[core, group], PROP_X + d, ((px + d) % nx * ny + py, om))
        pending.append((abuf.at[0, pl.ds(0, ny)], PROP_X + d))
    cross(0)
    each(nmode, functools.partial(send_entries, 1))
    pending.append((got.at[1, pl.ds(0, nmode - 1)], ENTRY + 1))

    loads[2].wait()
    loads[3].wait()
    for part in range(2):
        hb[part, pz, core] = bare[part] + field_weight * dens[part]
        hb[2 + part, pz, core] = dens[part]
    each(nz, send_fields)
    pending.append((hb.at[:, pl.ds(0, nz - 1), 0], FIELD_Z))
    for h in range(2):
        got[h, mu] = stage[h, mu]

    def sums_z(which, row):
        zbuf[which, pz] = row

        def send_sums(k):
            target = (mu, (pz + k) % nz * CORES + core)
            push(zbuf.at[which, pz], zbuf.at[which, pz], SUM_Z + which, target)

        each(nz, send_sums)
        pending.append((zbuf.at[which, pl.ds(0, nz - 1)], SUM_Z + which))

    def sums_y(which):
        arrive(zbuf.at[which, pl.ds(0, nz - 1)], SUM_Z + which)
        sd[which, core, mu] = zbuf[which][:, 0, :]

        def send_sums(k):
            target = (px * ny + (py + k) % ny, om)
            push(sd.at[which, core, mu], sd.at[which, core, mu], SUM_Y + which, target)

        each(ny, send_sums)
        pending.append((sd.at[which, 0, pl.ds(0, ny - 1)], SUM_Y + which))

    def sums_x(which):
        arrive(sd.at[which, 0, pl.ds(0, ny - 1)], SUM_Y + which)

        def send_sums(k):
            target = ((px + k) % nx * ny + py, om)
            push(sd.at[which, core, group], sd.at[which, core, group], SUM_X + which, target)

        each(nx, send_sums)
        pending.append((sd.at[which, 0, pl.ds(0, (nx - 1) * ny)], SUM_X + which))

    def sums_core(which):
        arrive(sd.at[which, 0, pl.ds(0, (nx - 1) * ny)], SUM_X + which)
        push(sd.at[which, core], sd.at[which, core], SUM_C + which, (mu, pair))
        pending.append((sd.at[which, 0], SUM_C + which))

    def sums_all(which):
        arrive(sd.at[which, 0], SUM_C + which)
        for side in range(2):
            for part in range(2):
                block = jnp.swapaxes(sd[which, side, part * rows : (part + 1) * rows], 0, 1)
                summed[part, :, side] = block
        return tuple(summed[part].reshape(size, size) for part in range(2))

    arrive(shared.at[pl.ds(0, nmode - 1)], FIRST)
    sums_z(0, jnp.sum(shared[:, :, :size], axis=0))
    for d in order[1:]:
        arrive(abuf.at[0, pl.ds(0, ny)], PROP_X + d)
        cross(d)
    sums_y(0)

    def matrix(part):
        return hb[part].reshape(size, size)

    def store_h(step, real, imag):
        rh, rl = split(time_step * real)
        ih, il = split(time_step * imag)
        for level, (r, i) in enumerate(((rh, ih), (rl, il))):
            hl[step, level, :size, :size] = r
            hl[step, level, size:, size:] = r
            hl[step, level, :size, size:] = -i
            hl[step, level, size:, :size] = i
            hr[step, level, :size, :size] = r
            hr[step, level, size:, size:] = r
            hr[step, level, :size, size:] = i
            hr[step, level, size:, :size] = -i

    def turn(step, real, imag):
        rh, rl = split(real)
        ih, il = split(imag)
        left = dot3(
            (hl[step, 0], hl[step, 1]),
            (jnp.concatenate([rh, ih], 0), jnp.concatenate([rl, il], 0)),
        )
        right = dot3(
            (jnp.concatenate([rh, ih], 1), jnp.concatenate([rl, il], 1)),
            (hr[step, 0], hr[step, 1]),
        )
        return (
            real + (left[size:] - right[:, size:]),
            imag - (left[:size] - right[:, :size]),
        )

    def unpack(d):
        arrive(abuf.at[0, pl.ds(0, ny)], PROP_C + d)

        def step(j, carry):
            k = (px - d + nx) % nx * ny + j
            block = jnp.concatenate([abuf[0, k], abuf[1, k]], 0)
            high, low = split(block)
            where = pl.ds(pl.multiple_of(k * norb, norb), norb)
            ah[where, :] = high
            al[where, :] = low
            return carry

        lax.fori_loop(0, ny, step, 0)

    def mix(h):
        high, low = split(got[h].reshape(modes, cols))
        span = ny * norb
        for d in order:
            if h == 0:
                unpack(d)
            first = (px - d + nx) % nx
            where = pl.ds(pl.multiple_of(first * span, span), span)
            mixed[h, where, :] = dot3((ah[where, :], al[where, :]), (high, low))

        for side in range(2):
            start = sides[side] * half

            def send_part(k):
                nu = (mu + k) % nmode
                rows_of = pl.ds(pl.multiple_of(nu * norb + start, half), half)
                there = back.at[h, mu, pl.ds(pl.multiple_of(start, half), half)]
                push(mixed.at[h, rows_of], there, (MIXED, NEAR_MIXED)[side] + h, (nu, om))

            each(nmode, send_part)
            pending.append((back.at[h, pl.ds(0, nmode - 1), pl.ds(0, half)], (MIXED, NEAR_MIXED)[side] + h))
        back[h, mu] = mixed[h, pl.ds(pl.multiple_of(mu * norb, norb), norb), :]

    arrive(got.at[0, pl.ds(0, nmode - 1)], ENTRY)
    mix(0)
    arrive(hb.at[:, pl.ds(0, nz - 1), 0], FIELD_Z)
    push(hb.at[:, :, core], hb.at[:, :, core], FIELD_C, (mu, pair))
    pending.append((hb.at[:, :, 0], FIELD_C))
    arrive(got.at[1, pl.ds(0, nmode - 1)], ENTRY + 1)
    mix(1)
    sums_x(0)
    tall = jnp.broadcast_to(shared[:, :, size:], (nmode, norb, LANES)).reshape(modes, LANES)
    at_lane = lax.broadcasted_iota(jnp.int32, (modes, LANES), 1)
    at_row = lax.broadcasted_iota(jnp.int32, (modes, LANES), 0)
    weights = jnp.dot(
        jnp.where(at_lane == at_row % norb, tall, 0.0), jnp.ones((LANES, LANES), F32),
        precision=lax.Precision.HIGHEST, preferred_element_type=F32,
    )
    wide = weights[:, :cols]
    own = prop[pl.ds(om, 1), :]
    sums_z(1, jnp.concatenate(
        [jnp.sum(wide * mixed[h], axis=0, keepdims=True) for h in range(2)], 1
    ))

    def spread_side(h, side):
        arrive(back.at[h, pl.ds(0, nmode - 1), pl.ds(0, half)], (MIXED, NEAR_MIXED)[side] + h)
        start = pl.multiple_of(sides[side] * half, half)
        block = jnp.swapaxes(back[h, :, pl.ds(start, half), :], 0, 1)
        stage2[h, pl.ds(start, half)] = block.reshape(half, 2, rows, cols)
        index = (WHOLE, NEAR_WHOLE)[side] + h

        def send_matrix(k):
            target = start + (om + k) % half
            push(stage2.at[h, target], whole.at[h, :, om], index, (mu, target))

        if side == 0:
            send_matrix(0)
        each(half, send_matrix)
        count = half - side
        pending.append((whole.at[h, :, pl.ds(0, count)], index))
        if side:
            whole[h, :, om] = stage2[h, om]

    spread_side(0, 0)
    spread_side(0, 1)
    sums_core(0)

    column = jnp.sum(weights[:, :1] * (ah[...].astype(F32) + al[...].astype(F32)), axis=0, keepdims=True)
    both = jnp.concatenate([own, column, jnp.zeros((6, modes), F32)], 0)
    products = jnp.dot(both, weights, precision=lax.Precision.HIGHEST, preferred_element_type=F32)
    e_own = products[0:1, 0:1]
    f_all = products[1:2, 0:1]
    c_all = jnp.sum(weights * weights, axis=0, keepdims=True)[:, :1]
    c_own = coup[om]
    arrive(hb.at[:, :, 0], FIELD_C)
    store_h(0, matrix(0), matrix(1))


    spread_side(1, 0)
    sums_y(1)
    spread_side(1, 1)
    sums_x(1)
    source = sums_all(0)
    densities = [(matrix(2), matrix(3))]
    fields = tuple(matrix(part) for part in range(2))
    for step in range(2):
        source = turn(step, *source)
        source = tuple(source[p] + (c_all * time_step) * densities[step][p] for p in range(2))
        densities.append(tuple(densities[step][p] + time_step * source[p] for p in range(2)))
        fields = tuple(fields[p] + (field_weight * time_step) * source[p] for p in range(2))
        store_h(step + 1, *fields)

    for h in range(2):
        arrive(whole.at[h, :, pl.ds(0, half)], WHOLE + h)
        arrive(whole.at[h, :, pl.ds(0, half - 1)], NEAR_WHOLE + h)
    state = tuple(
        jnp.concatenate([whole[h, part].reshape(size, cols) for h in range(2)], 1)
        for part in range(2)
    )
    for step in range(3):
        weight = e_own if step < 2 else c_own
        state = turn(step, *state)
        state = tuple(state[p] + (weight * time_step) * densities[step][p] for p in range(2))
    for part in range(2):
        final[part] = state[part].reshape(norb, rows, size)

    def send_result(k):
        target = (om + k) % norb
        push(final.at[:, target], out.at[om], RESULT, (mu, target))

    each(norb, send_result)
    pending.append((out.at[pl.ds(0, norb - 1)], RESULT))
    keep = pltpu.make_async_copy(final.at[:, om], out.at[om], load.at[0])
    keep.start()

    sums_core(1)
    chain = sums_all(1)
    for step in range(3):
        weight = f_all if step < 2 else c_all
        chain = turn(step, *chain)
        chain = tuple(chain[p] + (weight * time_step) * densities[step][p] for p in range(2))
    for part in range(2):
        summed[part] = (densities[2][part] + time_step * chain[part]).reshape(nz, CORES, rows, size)
    for part in range(2):
        dout[part] = summed[part, pz, core]

    keep.wait()
    arrive(out.at[pl.ds(0, norb - 1)], RESULT)
    for ref, index in pending:
        wait_for(ref, send.at[index])


def build(mesh, nx, ny):
    def on_device(correlators, density, bare_hamiltonian, coupling, propagator):
        local, _, rows, size = correlators.shape
        nmode, norb = mesh.shape["mode"], mesh.shape["orb"]
        nz = norb // CORES
        modes = nmode * norb
        vmem = pl.BlockSpec(memory_space=pltpu.VMEM)
        whole = pl.BlockSpec(memory_space=pltpu.HBM)
        return pl.pallas_call(
            functools.partial(kernel, (nx, ny, nz, rows, size)),
            out_shape=(
                jax.ShapeDtypeStruct(correlators.shape, F32),
                jax.ShapeDtypeStruct(density.shape, F32),
            ),
            in_specs=[whole, whole, whole, pl.BlockSpec(memory_space=pltpu.SMEM), whole],
            out_specs=(whole, vmem),
            scratch_shapes=[
                pltpu.VMEM((local, 2 * rows, size), F32),
                pltpu.VMEM(density.shape, F32),
                pltpu.VMEM(density.shape, F32),
                pltpu.VMEM(propagator.shape, F32),
                pltpu.VMEM((2, nmode, norb, size // 2), F32),
                pltpu.VMEM((2, nmode, norb, size // 2), F32),
                pltpu.VMEM((2, nmode, norb // 2, modes), F32),
                pltpu.VMEM((modes, modes), BF16),
                pltpu.VMEM((modes, modes), BF16),
                pltpu.VMEM((4, nz, CORES, rows, size), F32),
                pltpu.VMEM((2, nz, 1, size), F32),
                pltpu.VMEM((nmode, 1, size + LANES), F32),
                pltpu.VMEM((nmode, 1, size + LANES), F32),
                pltpu.VMEM((2, 2, nmode, nz, size), F32),
                pltpu.VMEM((2, modes, size // 2), F32),
                pltpu.VMEM((2, nmode, norb, size // 2), F32),
                pltpu.VMEM((2, norb, 2, rows, size // 2), F32),
                pltpu.VMEM((2, 2, norb, rows, size // 2), F32),
                pltpu.VMEM((2, norb, rows, size), F32),
                pltpu.VMEM((2, nz, CORES, rows, size), F32),
                pltpu.VMEM((3, 2, 2 * size, 2 * size), BF16),
                pltpu.VMEM((3, 2, 2 * size, 2 * size), BF16),
                pltpu.SemaphoreType.DMA((2 * nx + 22,)),
                pltpu.SemaphoreType.DMA((2 * nx + 22,)),
                pltpu.SemaphoreType.DMA((4,)),
            ],
            compiler_params=pltpu.CompilerParams(
                collective_id=0, has_side_effects=True, vmem_limit_bytes=60 * 1024 * 1024
            ),
        )(
            correlators.reshape(local, 2 * rows, size),
            density, bare_hamiltonian, coupling, propagator,
        )

    in_specs = (
        P("mode", None, "orb", None),
        P(None, "orb", None),
        P(None, "orb", None),
        P("mode"),
        P("mode", None),
    )
    out_specs = (P("mode", None, "orb", None), P(None, "orb", None))
    return jax.shard_map(
        on_device, mesh=mesh, in_specs=in_specs, out_specs=out_specs, check_vma=False
    )


def solution(mesh):
    return build(mesh, 4, mesh.shape["mode"] // 4)
```

```python
import functools

import jax
import jax.numpy as jnp
from jax import lax
from jax.experimental import pallas as pl
from jax.experimental.pallas import tpu as pltpu
from jax.sharding import PartitionSpec as P

MESH = pl.DeviceIdType.MESH
time_step = 0.1
field_weight = 0.0625
LANES = 128
CORES = 2
F32 = jnp.float32
BF16 = jnp.bfloat16


def split(value):
    high = value.astype(BF16)
    return high, (value - high.astype(F32)).astype(BF16)


def dot(first, second):
    return jnp.dot(first, second, preferred_element_type=F32)


def dot3(first, second):
    return dot(first[0], second[0]) + (dot(first[0], second[1]) + dot(first[1], second[0]))


def wait_for(ref, sem):
    pltpu.make_async_copy(ref, ref, sem).wait()


def kernel(
    dims,
    gin_hbm, dens_hbm, bare_hbm, coup, prop_hbm,
    out, dout,
    gin, dens, bare, prop, stage, got, abuf, ah, al, hb, zbuf, shares, shared, sd, mixed, back, stage2, whole, final, summed, hl, hr,
    send, recv, load,
):
    nx, ny, nz, rows, size = dims
    nmode, norb = nx * ny, nz * CORES
    modes = nmode * norb
    half = norb // 2
    cols = size // 2
    PROP_Y, PROP_X, PROP_C = 0, 0, nx
    base = 2 * nx
    ENTRY, MIXED, WHOLE = base, base + 2, base + 4
    FIELD_Z, FIELD_C, RESULT, FIRST = base + 6, base + 7, base + 8, base + 9
    SUM_Z, SUM_Y, SUM_X, SUM_C = base + 10, base + 12, base + 14, base + 16
    NEAR_MIXED, NEAR_WHOLE = base + 18, base + 20
    mu, om = lax.axis_index("mode"), lax.axis_index("orb")
    px, py = mu // ny, mu % ny
    pz, core = om // CORES, om % CORES
    other = 1 - core
    pair = pz * CORES + other

    def push(src, dst, index, target):
        pltpu.make_async_remote_copy(
            src_ref=src, dst_ref=dst, send_sem=send.at[index], recv_sem=recv.at[index],
            device_id=target, device_id_type=MESH,
        ).start()

    pending = []

    def arrive(ref, index):
        wait_for(ref, recv.at[index])

    def each(count, body):
        def step(k, carry):
            body(k)
            return carry
        lax.fori_loop(1, count, step, 0)

    loads = [
        pltpu.make_async_copy(src, dst, load.at[i])
        for i, (src, dst) in enumerate(
            ((prop_hbm, prop), (gin_hbm, gin), (bare_hbm, bare), (dens_hbm, dens))
        )
    ]
    for copy in loads:
        copy.start()

    barrier = pltpu.get_barrier_semaphore()

    def greet_mode(k):
        pl.semaphore_signal(barrier, inc=1, device_id=((mu + k) % nmode, om), device_id_type=MESH)

    def greet_orb(k):
        pl.semaphore_signal(barrier, inc=1, device_id=(mu, (om + k) % norb), device_id_type=MESH)

    each(nmode, greet_mode)
    each(norb, greet_orb)

    loads[0].wait()
    abuf[core, mu] = prop[pl.ds(pl.multiple_of(core * half, half), half), :]
    pl.semaphore_wait(barrier, nmode + norb - 2)

    def send_prop_y(k):
        push(abuf.at[core, mu], abuf.at[core, mu], PROP_Y, (px * ny + (py + k) % ny, om))

    each(ny, send_prop_y)
    pending.append((abuf.at[0, pl.ds(0, ny - 1)], PROP_Y))

    def send_entries(h, k):
        nu = (mu + k) % nmode
        push(stage.at[h, nu], got.at[h, mu], ENTRY + h, (nu, om))

    def send_fields(k):
        target = (pz + k) % nz
        push(hb.at[:, pz, core], hb.at[:, pz, core], FIELD_Z, (mu, target * CORES + core))

    loads[1].wait()
    share = coup[0] * gin[0]
    for i in range(1, norb):
        share = share + coup[i] * gin[i]
    lanes = lax.broadcasted_iota(jnp.int32, (nmode, LANES), 1)
    line = jnp.zeros((nmode, LANES), F32)
    for i in range(norb):
        line = jnp.where(lanes == i, coup[i], line)
    shares[...] = jnp.concatenate([share, line], 1)[:, None, :]

    def send_share(k):
        nu = (mu + k) % nmode
        push(shares.at[nu], shared.at[mu], FIRST, (nu, om))

    each(nmode, send_share)
    pending.append((shared.at[pl.ds(0, nmode - 1)], FIRST))
    shared[mu] = shares[mu]
    for h in range(2):
        stage[h] = jnp.swapaxes(gin[:, :, h * cols : (h + 1) * cols], 0, 1)
        if h == 0:
            each(nmode, functools.partial(send_entries, 0))
    pending.append((got.at[0, pl.ds(0, nmode - 1)], ENTRY))

    def span_of(d):
        return pl.ds(pl.multiple_of((px - d + nx) % nx * ny, ny), ny)

    near = om // half
    sides = (1 - near, near)
    order = [0, 1] + list(range(nx - 1, 1, -1))
    group = span_of(0)

    def cross(d):
        push(abuf.at[core, span_of(d)], abuf.at[core, span_of(d)], PROP_C + d, (mu, pair))
        pending.append((abuf.at[0, pl.ds(0, ny)], PROP_C + d))

    arrive(abuf.at[0, pl.ds(0, ny - 1)], PROP_Y)
    for d in order[1:]:
        push(abuf.at[core, group], abuf.at[core, group], PROP_X + d, ((px + d) % nx * ny + py, om))
        pending.append((abuf.at[0, pl.ds(0, ny)], PROP_X + d))
    cross(0)
    each(nmode, functools.partial(send_entries, 1))
    pending.append((got.at[1, pl.ds(0, nmode - 1)], ENTRY + 1))

    loads[2].wait()
    loads[3].wait()
    for part in range(2):
        hb[part, pz, core] = bare[part] + field_weight * dens[part]
        hb[2 + part, pz, core] = dens[part]
    each(nz, send_fields)
    pending.append((hb.at[:, pl.ds(0, nz - 1), 0], FIELD_Z))
    for h in range(2):
        got[h, mu] = stage[h, mu]

    def sums_z(which, row):
        zbuf[which, pz] = row

        def send_sums(k):
            target = (mu, (pz + k) % nz * CORES + core)
            push(zbuf.at[which, pz], zbuf.at[which, pz], SUM_Z + which, target)

        each(nz, send_sums)
        pending.append((zbuf.at[which, pl.ds(0, nz - 1)], SUM_Z + which))

    def sums_y(which):
        arrive(zbuf.at[which, pl.ds(0, nz - 1)], SUM_Z + which)
        sd[which, core, mu] = zbuf[which][:, 0, :]

        def send_sums(k):
            target = (px * ny + (py + k) % ny, om)
            push(sd.at[which, core, mu], sd.at[which, core, mu], SUM_Y + which, target)

        each(ny, send_sums)
        pending.append((sd.at[which, 0, pl.ds(0, ny - 1)], SUM_Y + which))

    def sums_x(which):
        arrive(sd.at[which, 0, pl.ds(0, ny - 1)], SUM_Y + which)

        def send_sums(k):
            target = ((px + k) % nx * ny + py, om)
            push(sd.at[which, core, group], sd.at[which, core, group], SUM_X + which, target)

        each(nx, send_sums)
        pending.append((sd.at[which, 0, pl.ds(0, (nx - 1) * ny)], SUM_X + which))

    def sums_core(which):
        arrive(sd.at[which, 0, pl.ds(0, (nx - 1) * ny)], SUM_X + which)
        push(sd.at[which, core], sd.at[which, core], SUM_C + which, (mu, pair))
        pending.append((sd.at[which, 0], SUM_C + which))

    def sums_all(which):
        arrive(sd.at[which, 0], SUM_C + which)
        for side in range(2):
            for part in range(2):
                block = jnp.swapaxes(sd[which, side, part * rows : (part + 1) * rows], 0, 1)
                summed[part, :, side] = block
        return tuple(summed[part].reshape(size, size) for part in range(2))

    arrive(shared.at[pl.ds(0, nmode - 1)], FIRST)
    sums_z(0, jnp.sum(shared[:, :, :size], axis=0))
    for d in order[1:]:
        arrive(abuf.at[0, pl.ds(0, ny)], PROP_X + d)
        cross(d)
    sums_y(0)

    def matrix(part):
        return hb[part].reshape(size, size)

    def store_h(step, real, imag):
        rh, rl = split(time_step * real)
        ih, il = split(time_step * imag)
        for level, (r, i) in enumerate(((rh, ih), (rl, il))):
            hl[step, level, :size, :size] = r
            hl[step, level, size:, size:] = r
            hl[step, level, :size, size:] = -i
            hl[step, level, size:, :size] = i
            hr[step, level, :size, :size] = r
            hr[step, level, size:, size:] = r
            hr[step, level, :size, size:] = i
            hr[step, level, size:, :size] = -i

    def turn(step, real, imag):
        rh, rl = split(real)
        ih, il = split(imag)
        left = dot3(
            (hl[step, 0], hl[step, 1]),
            (jnp.concatenate([rh, ih], 0), jnp.concatenate([rl, il], 0)),
        )
        right = dot3(
            (jnp.concatenate([rh, ih], 1), jnp.concatenate([rl, il], 1)),
            (hr[step, 0], hr[step, 1]),
        )
        return (
            real + (left[size:] - right[:, size:]),
            imag - (left[:size] - right[:, :size]),
        )

    def unpack(d):
        arrive(abuf.at[0, pl.ds(0, ny)], PROP_C + d)

        def step(j, carry):
            k = (px - d + nx) % nx * ny + j
            block = jnp.concatenate([abuf[0, k], abuf[1, k]], 0)
            high, low = split(block)
            where = pl.ds(pl.multiple_of(k * norb, norb), norb)
            ah[where, :] = high
            al[where, :] = low
            return carry

        lax.fori_loop(0, ny, step, 0)

    def mix(h):
        high, low = split(got[h].reshape(modes, cols))
        span = ny * norb
        for d in order:
            if h == 0:
                unpack(d)
            first = (px - d + nx) % nx
            where = pl.ds(pl.multiple_of(first * span, span), span)
            mixed[h, where, :] = dot3((ah[where, :], al[where, :]), (high, low))

        for side in range(2):
            start = sides[side] * half

            def send_part(k):
                nu = (mu + k) % nmode
                rows_of = pl.ds(pl.multiple_of(nu * norb + start, half), half)
                there = back.at[h, mu, pl.ds(pl.multiple_of(start, half), half)]
                push(mixed.at[h, rows_of], there, (MIXED, NEAR_MIXED)[side] + h, (nu, om))

            each(nmode, send_part)
            pending.append((back.at[h, pl.ds(0, nmode - 1), pl.ds(0, half)], (MIXED, NEAR_MIXED)[side] + h))
        back[h, mu] = mixed[h, pl.ds(pl.multiple_of(mu * norb, norb), norb), :]

    arrive(got.at[0, pl.ds(0, nmode - 1)], ENTRY)
    mix(0)
    arrive(hb.at[:, pl.ds(0, nz - 1), 0], FIELD_Z)
    push(hb.at[:, :, core], hb.at[:, :, core], FIELD_C, (mu, pair))
    pending.append((hb.at[:, :, 0], FIELD_C))
    arrive(got.at[1, pl.ds(0, nmode - 1)], ENTRY + 1)
    mix(1)
    sums_x(0)
    tall = jnp.broadcast_to(shared[:, :, size:], (nmode, norb, LANES)).reshape(modes, LANES)
    at_lane = lax.broadcasted_iota(jnp.int32, (modes, LANES), 1)
    at_row = lax.broadcasted_iota(jnp.int32, (modes, LANES), 0)
    weights = jnp.dot(
        jnp.where(at_lane == at_row % norb, tall, 0.0), jnp.ones((LANES, LANES), F32),
        precision=lax.Precision.HIGHEST, preferred_element_type=F32,
    )
    wide = weights[:, :cols]
    own = prop[pl.ds(om, 1), :]
    sums_z(1, jnp.concatenate(
        [jnp.sum(wide * mixed[h], axis=0, keepdims=True) for h in range(2)], 1
    ))

    def spread_side(h, side):
        arrive(back.at[h, pl.ds(0, nmode - 1), pl.ds(0, half)], (MIXED, NEAR_MIXED)[side] + h)
        start = pl.multiple_of(sides[side] * half, half)
        block = jnp.swapaxes(back[h, :, pl.ds(start, half), :], 0, 1)
        stage2[h, pl.ds(start, half)] = block.reshape(half, 2, rows, cols)
        index = (WHOLE, NEAR_WHOLE)[side] + h

        def send_matrix(k):
            target = start + (om + k) % half
            push(stage2.at[h, target], whole.at[h, :, om], index, (mu, target))

        if side == 0:
            send_matrix(0)
        each(half, send_matrix)
        count = half - side
        pending.append((whole.at[h, :, pl.ds(0, count)], index))
        if side:
            whole[h, :, om] = stage2[h, om]


    column = jnp.sum(weights[:, :1] * (ah[...].astype(F32) + al[...].astype(F32)), axis=0, keepdims=True)
    both = jnp.concatenate([own, column, jnp.zeros((6, modes), F32)], 0)
    products = jnp.dot(both, weights, precision=lax.Precision.HIGHEST, preferred_element_type=F32)
    e_own = products[0:1, 0:1]
    f_all = products[1:2, 0:1]
    c_all = jnp.sum(weights * weights, axis=0, keepdims=True)[:, :1]
    c_own = coup[om]
    arrive(hb.at[:, :, 0], FIELD_C)
    store_h(0, matrix(0), matrix(1))
    spread_side(0, 0)
    spread_side(0, 1)
    sums_core(0)


    spread_side(1, 0)
    sums_y(1)
    spread_side(1, 1)
    sums_x(1)
    source = sums_all(0)
    densities = [(matrix(2), matrix(3))]
    fields = tuple(matrix(part) for part in range(2))
    for step in range(2):
        source = turn(step, *source)
        source = tuple(source[p] + (c_all * time_step) * densities[step][p] for p in range(2))
        densities.append(tuple(densities[step][p] + time_step * source[p] for p in range(2)))
        fields = tuple(fields[p] + (field_weight * time_step) * source[p] for p in range(2))
        store_h(step + 1, *fields)

    for h in range(2):
        arrive(whole.at[h, :, pl.ds(0, half)], WHOLE + h)
        arrive(whole.at[h, :, pl.ds(0, half - 1)], NEAR_WHOLE + h)
    state = tuple(
        jnp.concatenate([whole[h, part].reshape(size, cols) for h in range(2)], 1)
        for part in range(2)
    )
    for step in range(2):
        state = turn(step, *state)
        state = tuple(state[p] + (e_own * time_step) * densities[step][p] for p in range(2))
    for part in range(2):
        final[part] = state[part].reshape(norb, rows, size)
        summed[part] = densities[2][part].reshape(nz, CORES, rows, size)
    stacked = split(jnp.concatenate(state, 0))
    span = half * rows
    for side in range(2):
        blocks = pl.ds(pl.multiple_of(sides[side] * half, half), half)
        lines = pl.ds(pl.multiple_of(sides[side] * span, span), span)
        lower = pl.ds(pl.multiple_of(size + sides[side] * span, span), span)
        layers = pl.ds(sides[side] * (nz // 2), nz // 2)
        own_rows = tuple(final[part, blocks].reshape(span, size) for part in range(2))
        left = tuple(dot3((hl[2, 0, at, :], hl[2, 1, at, :]), stacked) for at in (lines, lower))
        right = dot3(split(jnp.concatenate(own_rows, 1)), (hr[2, 0], hr[2, 1]))
        change = (left[1] - right[:, size:], right[:, :size] - left[0])
        for part in range(2):
            value = own_rows[part] + change[part]
            value = value + (c_own * time_step) * summed[part, layers].reshape(span, size)
            final[part, blocks] = value.reshape(half, rows, size)

        def send_result(k):
            target = sides[side] * half + (om + k) % half
            push(final.at[:, target], out.at[om], RESULT, (mu, target))

        if side == 0:
            send_result(0)
        each(half, send_result)
    pending.append((out.at[pl.ds(0, norb - 1)], RESULT))
    keep = pltpu.make_async_copy(final.at[:, om], out.at[om], load.at[0])
    keep.start()

    sums_core(1)
    chain = sums_all(1)
    for step in range(3):
        weight = f_all if step < 2 else c_all
        chain = turn(step, *chain)
        chain = tuple(chain[p] + (weight * time_step) * densities[step][p] for p in range(2))
    for part in range(2):
        summed[part] = (densities[2][part] + time_step * chain[part]).reshape(nz, CORES, rows, size)
    for part in range(2):
        dout[part] = summed[part, pz, core]

    keep.wait()
    arrive(out.at[pl.ds(0, norb - 1)], RESULT)
    for ref, index in pending:
        wait_for(ref, send.at[index])


def build(mesh, nx, ny):
    def on_device(correlators, density, bare_hamiltonian, coupling, propagator):
        local, _, rows, size = correlators.shape
        nmode, norb = mesh.shape["mode"], mesh.shape["orb"]
        nz = norb // CORES
        modes = nmode * norb
        vmem = pl.BlockSpec(memory_space=pltpu.VMEM)
        whole = pl.BlockSpec(memory_space=pltpu.HBM)
        return pl.pallas_call(
            functools.partial(kernel, (nx, ny, nz, rows, size)),
            out_shape=(
                jax.ShapeDtypeStruct(correlators.shape, F32),
                jax.ShapeDtypeStruct(density.shape, F32),
            ),
            in_specs=[whole, whole, whole, pl.BlockSpec(memory_space=pltpu.SMEM), whole],
            out_specs=(whole, vmem),
            scratch_shapes=[
                pltpu.VMEM((local, 2 * rows, size), F32),
                pltpu.VMEM(density.shape, F32),
                pltpu.VMEM(density.shape, F32),
                pltpu.VMEM(propagator.shape, F32),
                pltpu.VMEM((2, nmode, norb, size // 2), F32),
                pltpu.VMEM((2, nmode, norb, size // 2), F32),
                pltpu.VMEM((2, nmode, norb // 2, modes), F32),
                pltpu.VMEM((modes, modes), BF16),
                pltpu.VMEM((modes, modes), BF16),
                pltpu.VMEM((4, nz, CORES, rows, size), F32),
                pltpu.VMEM((2, nz, 1, size), F32),
                pltpu.VMEM((nmode, 1, size + LANES), F32),
                pltpu.VMEM((nmode, 1, size + LANES), F32),
                pltpu.VMEM((2, 2, nmode, nz, size), F32),
                pltpu.VMEM((2, modes, size // 2), F32),
                pltpu.VMEM((2, nmode, norb, size // 2), F32),
                pltpu.VMEM((2, norb, 2, rows, size // 2), F32),
                pltpu.VMEM((2, 2, norb, rows, size // 2), F32),
                pltpu.VMEM((2, norb, rows, size), F32),
                pltpu.VMEM((2, nz, CORES, rows, size), F32),
                pltpu.VMEM((3, 2, 2 * size, 2 * size), BF16),
                pltpu.VMEM((3, 2, 2 * size, 2 * size), BF16),
                pltpu.SemaphoreType.DMA((2 * nx + 22,)),
                pltpu.SemaphoreType.DMA((2 * nx + 22,)),
                pltpu.SemaphoreType.DMA((4,)),
            ],
            compiler_params=pltpu.CompilerParams(
                collective_id=0, has_side_effects=True, vmem_limit_bytes=60 * 1024 * 1024
            ),
        )(
            correlators.reshape(local, 2 * rows, size),
            density, bare_hamiltonian, coupling, propagator,
        )

    in_specs = (
        P("mode", None, "orb", None),
        P(None, "orb", None),
        P(None, "orb", None),
        P("mode"),
        P("mode", None),
    )
    out_specs = (P("mode", None, "orb", None), P(None, "orb", None))
    return jax.shard_map(
        on_device, mesh=mesh, in_specs=in_specs, out_specs=out_specs, check_vma=False
    )


def solution(mesh):
    return build(mesh, 4, mesh.shape["mode"] // 4)
```
